32 devices in a mesh: illum: 2 (over y), slab: 16 (over z, x, core).
Axes of the slice: x: 2, y: 2, z: 4, core: 2. Of those that a mesh axis runs over, the one named last changes fastest.
Arguments:
- incident: bfloat16 [2, 2, 64, 256, 128], P('illum', None, 'slab'), may hold values from -6 to 6
- field_now: float32 [2, 2, 64, 256, 128], P('illum', None, 'slab'), may hold values from -6 to 6
- contrast: float32 [64, 256, 128], P('slab'), may hold values from 0 to 0.5
- green_spectrum: float32 [2, 64, 256, 128], P(None, None, 'slab'), may hold values from -6 to 6
- detector_data: float32 [2, 2, 256, 128], P('illum', None, 'slab'), may hold values from -6 to 6
Outputs:
- field_next: float32 [2, 2, 64, 256, 128], P('illum', None, 'slab')
- misfit: float32 [2, 2, 256, 128], P('illum', None, 'slab')
- contrast_next: float32 [64, 256, 128], P('slab')
The draws below stay inside these ranges and needn't reach their ends.
All inputs are finite; a program needn't handle non-finite values.
Results may differ from the reference program's by a relative error of at most 0.0003.
Values sent between devices are 32-bit elements; how exact they have to be, the bound alone decides.
A program may use at most 64 MiB of HBM per device.

```python
import math
import jax
import jax.numpy as jnp
from jax import lax

NX = 256
NY = 128
NZ = 64
ILLUMS = 2


def draw_field_now(key, part):
    plane_key = jax.random.fold_in(key, 7101)
    rough_key = jax.random.fold_in(key, 7102)
    common_plane = jnp.clip(jax.random.normal(plane_key, (ILLUMS, 2, 1, NX, NY), jnp.float32), -4.0, 4.0)
    rough_part = jnp.clip(jax.random.normal(rough_key, (ILLUMS, 2, NZ, NX, NY), jnp.float32), -4.0, 4.0)
    return 0.8 * common_plane + 0.6 * rough_part


def draw_contrast(key, part):
    plane_key = jax.random.fold_in(key, 8201)
    rough_key = jax.random.fold_in(key, 8202)
    common_plane = jax.random.uniform(plane_key, (1, NX, NY), jnp.float32, 0.0, 1.0)
    rough_part = jax.random.uniform(rough_key, (NZ, NX, NY), jnp.float32, 0.0, 1.0)
    return 0.5 * (0.6 * common_plane + 0.4 * rough_part)


def steps_of(rng, extent, pieces, smallest, largest):
    factor_of, own = 1.0, jax.random.fold_in(rng, 6)
    for axis_at, parts in pieces:
        steps = jnp.exp(jax.random.uniform(jax.random.fold_in(own, axis_at), (parts,), jnp.float32, smallest / len(pieces), largest / len(pieces)))
        factor_of = factor_of * jnp.repeat(steps, extent[axis_at] // parts).reshape([-1 if axis == axis_at else 1 for axis in range(len(extent))])
    return factor_of


def centred(stream_key, shape, spread, bound, cuts=(), held_as=jnp.bfloat16):
    result = jax.random.normal(stream_key, shape, jnp.float32) * spread
    if len(cuts) > 0:
        result = steps_of(stream_key, shape, cuts, -0.22, 0.18) * result
    return jnp.clip(result, min=-bound, max=bound).astype(held_as)


def setup_inputs(seed: int = 0) -> dict:
    splits = jax.random.split(jax.random.key(seed), 6)
    incident = centred(splits[0], (ILLUMS, 2, NZ, NX, NY), 1.0, 6.0, ((0, 2), (2, 16)))
    field_now = draw_field_now(jax.random.fold_in(splits[5], 71), 0)
    contrast = draw_contrast(jax.random.fold_in(splits[5], 71), 0)
    green_spectrum = centred(splits[3], (2, NZ, NX, NY), 1.0, 6.0, ((2, 16),), jnp.float32)
    detector_data = centred(splits[4], (ILLUMS, 2, NX, NY), 1.0, 6.0, ((0, 2), (2, 16)), jnp.float32)
    return {"incident": incident, "field_now": field_now, "contrast": contrast, "green_spectrum": green_spectrum, "detector_data": detector_data}


wave_number = 1.2
step_size = 2.0
diffusion = 0.02
edge_scale = 0.25

def frequency(index, length):
    shifted = jnp.where(index < length // 2, index, index - length)
    return shifted.astype(jnp.float32) * (2.0 * math.pi / length)

def propagator(depth_index, row_index, width_x, width_y, depth):
    along_x = frequency(row_index, width_x)
    along_y = frequency(jnp.arange(width_y, dtype=jnp.int32), width_y)
    squared = wave_number ** 2 - along_x[None, :, None] ** 2 - along_y[None, None, :] ** 2
    distance = (depth - depth_index).astype(jnp.float32)[:, None, None]
    root = jnp.sqrt(jnp.abs(squared))
    moving = squared > 0.0
    amplitude = jnp.where(moving, 1.0, jnp.exp(-root * distance))
    phase = jnp.where(moving, root * distance, 0.0)
    return (amplitude * jnp.cos(phase), amplitude * jnp.sin(phase))

def tv_pass(padded, first, depth):
    rows = padded.shape[0]
    global_row = first + jnp.arange(rows - 1, dtype=jnp.int32)
    inside = (global_row >= 0) & (global_row <= depth - 2)
    core = padded[:-1]
    slope_depth = jnp.where(inside[:, None, None], padded[1:] - core, 0.0)
    slope_rows = jnp.concatenate([core[:, 1:] - core[:, :-1], jnp.zeros_like(core[:, :1])], axis=1)
    slope_cols = jnp.concatenate([core[:, :, 1:] - core[:, :, :-1], jnp.zeros_like(core[:, :, :1])], axis=2)
    magnitude = jnp.sqrt(slope_depth ** 2 + slope_rows ** 2 + slope_cols ** 2 + edge_scale ** 2)
    flux_depth = slope_depth / magnitude
    flux_rows = (slope_rows / magnitude)[1:]
    flux_cols = (slope_cols / magnitude)[1:]
    spread_depth = flux_depth[1:] - flux_depth[:-1]
    spread_rows = flux_rows - jnp.concatenate([jnp.zeros_like(flux_rows[:, :1]), flux_rows[:, :-1]], axis=1)
    spread_cols = flux_cols - jnp.concatenate([jnp.zeros_like(flux_cols[:, :, :1]), flux_cols[:, :, :-1]], axis=2)
    return padded[1:-1] + diffusion * (spread_depth + spread_rows + spread_cols)

def reference(incident, field_now, contrast, green_spectrum, detector_data):
    cos_prop, sin_prop = propagator(jnp.arange(NZ, dtype=jnp.int32), jnp.arange(NX, dtype=jnp.int32), NX, NY, NZ)
    propagate = cos_prop + 1j * sin_prop
    green = green_spectrum[0] + 1j * green_spectrum[1]
    root_depth = math.sqrt(NZ)

    def per_angle(gradient, items):
        incoming, current, measured = items
        source = contrast * (current[0] + 1j * current[1])
        spectrum = jnp.fft.fft2(source, axes=(1, 2), norm='ortho')
        deep = jnp.fft.fft(spectrum, axis=0, norm='ortho')
        volume = jnp.fft.ifft(green * deep, axis=0, norm='ortho')
        scattered = jnp.fft.ifft2(volume, axes=(1, 2), norm='ortho')
        field_next = jnp.stack([incoming[0].astype(jnp.float32) + scattered.real, incoming[1].astype(jnp.float32) + scattered.imag])
        predicted = lax.optimization_barrier(jnp.sum(propagate * spectrum, axis=0)) / root_depth
        mismatch = predicted - (measured[0] + 1j * measured[1])
        returned = jnp.fft.ifft2(jnp.conj(propagate) * mismatch[None] / root_depth, axes=(1, 2), norm='ortho')
        gradient = gradient + current[0] * returned.real + current[1] * returned.imag
        return (gradient, (field_next, jnp.stack([mismatch.real, mismatch.imag])))
    gradient, outputs = lax.scan(per_angle, jnp.zeros_like(contrast), (incident, field_now, detector_data))
    fields, misfit = outputs
    updated = contrast - step_size * gradient
    for repeat in range(4):
        padded = jnp.pad(updated, ((1, 1), (0, 0), (0, 0)))
        updated = tv_pass(padded, -1, NZ)
    return (fields, misfit, updated)
```

```python
import math

import jax
import jax.numpy as jnp
from jax import lax
from jax.sharding import PartitionSpec as P

wave_number = 1.2
step_size = 2.0
diffusion = 0.02
edge_scale = 0.25
passes = 4
highest = lax.Precision.HIGH
form_rows = "...xy,xk->...ky"
form_cols = "...y,yk->...k"
form_depth = "azxy,zk->akxy"


def with_halo(array, sides, width):
    for axis, dim in sides:
        devices, length = (lax.axis_size(axis), array.shape[dim])
        up = [(i, (i + 1) % devices) for i in range(devices - 1)]
        down = [(j, i) for i, j in up]
        last = lax.slice_in_dim(array, length - width, length, axis=dim)
        leading = lax.slice_in_dim(array, 0, width, axis=dim)
        before = lax.ppermute(last, axis, up)
        after = lax.ppermute(leading, axis, down)
        array = jnp.concatenate([before, array, after], axis=dim)
    return array


def tables(length):
    counter = jnp.arange(length, dtype=jnp.int32)
    product = counter[:, None] * counter[None, :] % length
    angle = product.astype(jnp.float32) * (2.0 * math.pi / length)
    scale = 1.0 / math.sqrt(length)
    return (jnp.cos(angle) * scale, jnp.sin(angle) * scale)


def mixing(real, imag, cosine, sine_table, sign, form):
    real_cos = jnp.einsum(form, real, cosine, precision=highest)
    real_sin = jnp.einsum(form, real, sine_table, precision=highest)
    imag_cos = jnp.einsum(form, imag, cosine, precision=highest)
    imag_sin = jnp.einsum(form, imag, sine_table, precision=highest)
    return (real_cos - sign * imag_sin, imag_cos + sign * real_sin)


def frequency(index, length):
    shifted = jnp.where(index < length // 2, index, index - length)
    return shifted.astype(jnp.float32) * (2.0 * math.pi / length)


def propagator(depth_index, row_index, width_x, width_y, depth):
    along_x = frequency(row_index, width_x)
    along_y = frequency(jnp.arange(width_y, dtype=jnp.int32), width_y)
    squared = wave_number**2 - along_x[None, :, None] ** 2 - along_y[None, None, :] ** 2
    distance = (depth - depth_index).astype(jnp.float32)[:, None, None]
    root = jnp.sqrt(jnp.abs(squared))
    moving = squared > 0.0
    amplitude = jnp.where(moving, 1.0, jnp.exp(-root * distance))
    phase = jnp.where(moving, root * distance, 0.0)
    return (amplitude * jnp.cos(phase), amplitude * jnp.sin(phase))


def tv_pass(padded, first, depth):
    rows = padded.shape[0]
    global_row = first + jnp.arange(rows - 1, dtype=jnp.int32)
    inside = (global_row >= 0) & (global_row <= depth - 2)
    core = padded[:-1]
    slope_depth = jnp.where(inside[:, None, None], padded[1:] - core, 0.0)
    slope_rows = jnp.concatenate([core[:, 1:] - core[:, :-1], jnp.zeros_like(core[:, :1])], axis=1)
    slope_cols = jnp.concatenate(
        [core[:, :, 1:] - core[:, :, :-1], jnp.zeros_like(core[:, :, :1])], axis=2
    )
    magnitude = jnp.sqrt(slope_depth**2 + slope_rows**2 + slope_cols**2 + edge_scale**2)
    flux_depth = slope_depth / magnitude
    flux_rows = (slope_rows / magnitude)[1:]
    flux_cols = (slope_cols / magnitude)[1:]
    spread_depth = flux_depth[1:] - flux_depth[:-1]
    spread_rows = flux_rows - jnp.concatenate(
        [jnp.zeros_like(flux_rows[:, :1]), flux_rows[:, :-1]], axis=1
    )
    spread_cols = flux_cols - jnp.concatenate(
        [jnp.zeros_like(flux_cols[:, :, :1]), flux_cols[:, :, :-1]], axis=2
    )
    return padded[1:-1] + diffusion * (spread_depth + spread_rows + spread_cols)


def back_project(prop_real, prop_imag, mismatch, root_depth):
    miss_real = mismatch[:, 0][:, None]
    miss_imag = mismatch[:, 1][:, None]
    out_real = (prop_real[None] * miss_real + prop_imag[None] * miss_imag) / root_depth
    out_imag = (prop_real[None] * miss_imag - prop_imag[None] * miss_real) / root_depth
    return jnp.stack([out_real, out_imag], 1)


def shards(incident, field_now, contrast, green_spectrum, detector_data):
    slabs = lax.axis_size("slab")
    place = lax.axis_index("slab")
    local_depth, width_x, width_y = contrast.shape
    depth = local_depth * slabs
    cols_x = width_x // slabs
    root_depth = math.sqrt(depth)
    cos_x, sin_x = tables(width_x)
    cos_y, sin_y = tables(width_y)
    cos_z, sin_z = tables(depth)
    real_now = field_now[:, 0]
    imag_now = field_now[:, 1]
    spec_real, spec_imag = mixing(
        contrast[None] * real_now, contrast[None] * imag_now, cos_x, sin_x, -1.0, form_rows
    )
    spec_real, spec_imag = mixing(spec_real, spec_imag, cos_y, sin_y, -1.0, form_cols)
    spectrum = jnp.stack([spec_real, spec_imag], 1)
    columns = lax.all_to_all(spectrum, "slab", split_axis=3, concat_axis=2, tiled=True)
    deep_real, deep_imag = mixing(columns[:, 0], columns[:, 1], cos_z, sin_z, -1.0, form_depth)
    green_real = green_spectrum[0][None]
    green_imag = green_spectrum[1][None]
    prod_real = green_real * deep_real - green_imag * deep_imag
    prod_imag = green_real * deep_imag + green_imag * deep_real
    vol_real, vol_imag = mixing(prod_real, prod_imag, cos_z, sin_z, 1.0, form_depth)
    volume = jnp.stack([vol_real, vol_imag], 1)
    kx_index = place * cols_x + jnp.arange(cols_x, dtype=jnp.int32)
    col_prop_real, col_prop_imag = propagator(
        jnp.arange(depth, dtype=jnp.int32), kx_index, width_x, width_y, depth
    )
    col_real = columns[:, 0]
    col_imag = columns[:, 1]
    pred_real = (
        jnp.sum(col_prop_real[None] * col_real - col_prop_imag[None] * col_imag, axis=1)
        / root_depth
    )
    pred_imag = (
        jnp.sum(col_prop_real[None] * col_imag + col_prop_imag[None] * col_real, axis=1)
        / root_depth
    )
    mismatch = jnp.stack([pred_real, pred_imag], 1) - detector_data
    volume = lax.all_to_all(volume, "slab", split_axis=2, concat_axis=3, tiled=True)
    depth_index = place * local_depth + jnp.arange(local_depth, dtype=jnp.int32)
    prop_real, prop_imag = propagator(
        depth_index, jnp.arange(width_x, dtype=jnp.int32), width_x, width_y, depth
    )
    gathered = lax.all_gather(mismatch, "slab", axis=2, tiled=True)
    returned = back_project(prop_real, prop_imag, gathered, root_depth)
    scat_real, scat_imag = mixing(volume[:, 0], volume[:, 1], cos_x, sin_x, 1.0, form_rows)
    scat_real, scat_imag = mixing(scat_real, scat_imag, cos_y, sin_y, 1.0, form_cols)
    field_next = incident.astype(jnp.float32) + jnp.stack([scat_real, scat_imag], 1)
    ret_real, ret_imag = mixing(returned[:, 0], returned[:, 1], cos_x, sin_x, 1.0, form_rows)
    ret_real, ret_imag = mixing(ret_real, ret_imag, cos_y, sin_y, 1.0, form_cols)
    local_terms = jnp.sum(real_now * ret_real + imag_now * ret_imag, axis=0)
    illums = lax.axis_size("illum")
    gradient, travelling = local_terms, local_terms
    for hop in range(illums - 1):
        travelling = lax.ppermute(travelling, "illum", [(i, (i + 1) % illums) for i in range(illums)])
        gradient = gradient + travelling
    updated = contrast - step_size * gradient
    wide = math.gcd(passes, local_depth)
    for repeat in range(passes // wide):
        updated = with_halo(updated, (("slab", 0),), wide)
        for left in range(wide, 0, -1):
            updated = tv_pass(updated, place * local_depth - left, depth)
    return (field_next, mismatch, updated)


def solution(mesh):
    placed = (
        P("illum", None, "slab", None, None),
        P("illum", None, "slab", None, None),
        P("slab", None, None),
        P(None, None, "slab", None),
        P("illum", None, "slab", None),
    )
    return jax.shard_map(
        shards,
        mesh=mesh,
        in_specs=placed,
        out_specs=(
            P("illum", None, "slab", None, None),
            P("illum", None, "slab", None),
            P("slab", None, None),
        ),
        check_vma=False,
    )
```

```python
import math

import jax
import jax.numpy as jnp
import ml_dtypes
import numpy as np
from jax import lax
from jax.experimental import pallas as pl
from jax.experimental.pallas import tpu as pltpu
from jax.sharding import PartitionSpec as P

wave_number = 1.2
step_size = 2.0
diffusion = 0.02
edge_scale = 0.25
passes = 4
MESH = pl.DeviceIdType.MESH
highest = lax.Precision.HIGH
form_rows = "...xy,xk->...ky"
form_cols = "...y,yk->...k"
form_depth = "azxy,zk->akxy"


def with_halo(array, sides, width):
    for axis, dim in sides:
        devices, length = (lax.axis_size(axis), array.shape[dim])
        up = [(i, (i + 1) % devices) for i in range(devices - 1)]
        down = [(j, i) for i, j in up]
        last = lax.slice_in_dim(array, length - width, length, axis=dim)
        leading = lax.slice_in_dim(array, 0, width, axis=dim)
        before = lax.ppermute(last, axis, up)
        after = lax.ppermute(leading, axis, down)
        array = jnp.concatenate([before, array, after], axis=dim)
    return array


def tables(length):
    counter = jnp.arange(length, dtype=jnp.int32)
    product = counter[:, None] * counter[None, :] % length
    angle = product.astype(jnp.float32) * (2.0 * math.pi / length)
    scale = 1.0 / math.sqrt(length)
    return (jnp.cos(angle) * scale, jnp.sin(angle) * scale)


def mixing(real, imag, cosine, sine_table, sign, form):
    real_cos = jnp.einsum(form, real, cosine, precision=highest)
    real_sin = jnp.einsum(form, real, sine_table, precision=highest)
    imag_cos = jnp.einsum(form, imag, cosine, precision=highest)
    imag_sin = jnp.einsum(form, imag, sine_table, precision=highest)
    return (real_cos - sign * imag_sin, imag_cos + sign * real_sin)


def frequency(index, length):
    shifted = jnp.where(index < length // 2, index, index - length)
    return shifted.astype(jnp.float32) * (2.0 * math.pi / length)


def propagator(depth_index, row_index, width_x, width_y, depth):
    along_x = frequency(row_index, width_x)
    along_y = frequency(jnp.arange(width_y, dtype=jnp.int32), width_y)
    squared = wave_number**2 - along_x[None, :, None] ** 2 - along_y[None, None, :] ** 2
    distance = (depth - depth_index).astype(jnp.float32)[:, None, None]
    root = jnp.sqrt(jnp.abs(squared))
    moving = squared > 0.0
    amplitude = jnp.where(moving, 1.0, jnp.exp(-root * distance))
    phase = jnp.where(moving, root * distance, 0.0)
    return (amplitude * jnp.cos(phase), amplitude * jnp.sin(phase))


def tv_pass(padded, first, depth):
    rows = padded.shape[0]
    global_row = first + jnp.arange(rows - 1, dtype=jnp.int32)
    inside = (global_row >= 0) & (global_row <= depth - 2)
    core = padded[:-1]
    slope_depth = jnp.where(inside[:, None, None], padded[1:] - core, 0.0)
    slope_rows = jnp.concatenate([core[:, 1:] - core[:, :-1], jnp.zeros_like(core[:, :1])], axis=1)
    slope_cols = jnp.concatenate(
        [core[:, :, 1:] - core[:, :, :-1], jnp.zeros_like(core[:, :, :1])], axis=2
    )
    magnitude = jnp.sqrt(slope_depth**2 + slope_rows**2 + slope_cols**2 + edge_scale**2)
    flux_depth = slope_depth / magnitude
    flux_rows = (slope_rows / magnitude)[1:]
    flux_cols = (slope_cols / magnitude)[1:]
    spread_depth = flux_depth[1:] - flux_depth[:-1]
    spread_rows = flux_rows - jnp.concatenate(
        [jnp.zeros_like(flux_rows[:, :1]), flux_rows[:, :-1]], axis=1
    )
    spread_cols = flux_cols - jnp.concatenate(
        [jnp.zeros_like(flux_cols[:, :, :1]), flux_cols[:, :, :-1]], axis=2
    )
    return padded[1:-1] + diffusion * (spread_depth + spread_rows + spread_cols)


def back_project(prop_real, prop_imag, mismatch, root_depth):
    miss_real = mismatch[:, 0][:, None]
    miss_imag = mismatch[:, 1][:, None]
    out_real = (prop_real[None] * miss_real + prop_imag[None] * miss_imag) / root_depth
    out_imag = (prop_real[None] * miss_imag - prop_imag[None] * miss_real) / root_depth
    return jnp.stack([out_real, out_imag], 1)


def shards(incident, field_now, contrast, green_spectrum, detector_data):
    slabs = lax.axis_size("slab")
    place = lax.axis_index("slab")
    local_depth, width_x, width_y = contrast.shape
    depth = local_depth * slabs
    cols_x = width_x // slabs
    root_depth = math.sqrt(depth)
    cos_x, sin_x = tables(width_x)
    cos_y, sin_y = tables(width_y)
    cos_z, sin_z = tables(depth)
    real_now = field_now[:, 0]
    imag_now = field_now[:, 1]
    spec_real, spec_imag = mixing(
        contrast[None] * real_now, contrast[None] * imag_now, cos_x, sin_x, -1.0, form_rows
    )
    spec_real, spec_imag = mixing(spec_real, spec_imag, cos_y, sin_y, -1.0, form_cols)
    spectrum = jnp.stack([spec_real, spec_imag], 1)
    columns = lax.all_to_all(spectrum, "slab", split_axis=3, concat_axis=2, tiled=True)
    deep_real, deep_imag = mixing(columns[:, 0], columns[:, 1], cos_z, sin_z, -1.0, form_depth)
    green_real = green_spectrum[0][None]
    green_imag = green_spectrum[1][None]
    prod_real = green_real * deep_real - green_imag * deep_imag
    prod_imag = green_real * deep_imag + green_imag * deep_real
    vol_real, vol_imag = mixing(prod_real, prod_imag, cos_z, sin_z, 1.0, form_depth)
    volume = jnp.stack([vol_real, vol_imag], 1)
    kx_index = place * cols_x + jnp.arange(cols_x, dtype=jnp.int32)
    col_prop_real, col_prop_imag = propagator(
        jnp.arange(depth, dtype=jnp.int32), kx_index, width_x, width_y, depth
    )
    col_real = columns[:, 0]
    col_imag = columns[:, 1]
    pred_real = (
        jnp.sum(col_prop_real[None] * col_real - col_prop_imag[None] * col_imag, axis=1)
        / root_depth
    )
    pred_imag = (
        jnp.sum(col_prop_real[None] * col_imag + col_prop_imag[None] * col_real, axis=1)
        / root_depth
    )
    mismatch = jnp.stack([pred_real, pred_imag], 1) - detector_data
    volume = lax.all_to_all(volume, "slab", split_axis=2, concat_axis=3, tiled=True)
    depth_index = place * local_depth + jnp.arange(local_depth, dtype=jnp.int32)
    prop_real, prop_imag = propagator(
        depth_index, jnp.arange(width_x, dtype=jnp.int32), width_x, width_y, depth
    )
    gathered = lax.all_gather(mismatch, "slab", axis=2, tiled=True)
    returned = back_project(prop_real, prop_imag, gathered, root_depth)
    scat_real, scat_imag = mixing(volume[:, 0], volume[:, 1], cos_x, sin_x, 1.0, form_rows)
    scat_real, scat_imag = mixing(scat_real, scat_imag, cos_y, sin_y, 1.0, form_cols)
    field_next = incident.astype(jnp.float32) + jnp.stack([scat_real, scat_imag], 1)
    ret_real, ret_imag = mixing(returned[:, 0], returned[:, 1], cos_x, sin_x, 1.0, form_rows)
    ret_real, ret_imag = mixing(ret_real, ret_imag, cos_y, sin_y, 1.0, form_cols)
    local_terms = jnp.sum(real_now * ret_real + imag_now * ret_imag, axis=0)
    illums = lax.axis_size("illum")
    gradient, travelling = local_terms, local_terms
    for hop in range(illums - 1):
        travelling = lax.ppermute(travelling, "illum", [(i, (i + 1) % illums) for i in range(illums)])
        gradient = gradient + travelling
    updated = contrast - step_size * gradient
    wide = math.gcd(passes, local_depth)
    for repeat in range(passes // wide):
        updated = with_halo(updated, (("slab", 0),), wide)
        for left in range(wide, 0, -1):
            updated = tv_pass(updated, place * local_depth - left, depth)
    return (field_next, mismatch, updated)


def split_halves(value):
    high = value.astype(jnp.bfloat16)
    return high, (value - high.astype(jnp.float32)).astype(jnp.bfloat16)


def product(left, right):
    return jnp.dot(left, right, preferred_element_type=jnp.float32)


def combine(both, sign):
    rows, cols = both.shape[0] // 2, both.shape[1] // 2
    by_cos, by_sin = both[:rows], both[rows:]
    real = by_cos[:, :cols] - sign * by_sin[:, cols:]
    imag = by_cos[:, cols:] + sign * by_sin[:, :cols]
    return real, imag


def transform_rows(pair, high_ref, low_ref, sign):
    high, low = split_halves(pair)
    table = high_ref[...]
    both = product(table, high) + product(table, low) + product(low_ref[...], high)
    return jnp.concatenate(combine(both, sign), axis=1)


def transform_cols(pair, high_ref, low_ref):
    high, low = split_halves(pair)
    table = high_ref[...]
    return product(high, table) + product(low, table) + product(high, low_ref[...])


def host_split(table):
    table = table.astype(np.float32)
    high = table.astype(ml_dtypes.bfloat16)
    low = (table - high.astype(np.float32)).astype(ml_dtypes.bfloat16)
    return high, low


def host_tables(length):
    counter = np.arange(length)
    angle = (counter[:, None] * counter[None, :] % length) * (2.0 * math.pi / length)
    return np.cos(angle) / math.sqrt(length), np.sin(angle) / math.sqrt(length)


def host_frequency(length):
    index = np.arange(length)
    return np.where(index < length // 2, index, index - length) * (2.0 * math.pi / length)


def host_propagator(distance, width_x, width_y):
    squared = (
        wave_number**2 - host_frequency(width_x)[:, None] ** 2 - host_frequency(width_y)[None] ** 2
    )
    root = np.sqrt(np.abs(squared))
    moving = squared > 0.0
    amplitude = np.where(moving, 1.0, np.exp(-root * distance))
    phase = np.where(moving, root * distance, 0.0)
    pair = [amplitude * np.cos(phase), amplitude * np.sin(phase)]
    return np.concatenate(pair, axis=1).astype(np.float32)


def fused_kernel(
    field, contrast, detector, xh, xl, yfh, yfl, yih, yil, zt_ref, step_ref,
    incident_any, green_any, start_any,
    field_out, misfit_out, contrast_out,
    out1, in1, out2, in2, miss, gmine, gpeer, cube, cube2, zbuf, gbuf, rbuf, fz, inc, green, start,
    load_sem, s1, r1, s2, r2, sm, rm, sg, rg, sh, rh,
):
    slabs, local_depth, cols_x, pair_y = out1.shape
    width_y = pair_y // 2
    width_x = slabs * cols_x
    depth = slabs * local_depth
    root_depth = math.sqrt(depth)
    me = lax.axis_index("slab")
    lane = lax.axis_index("illum")
    other = 1 - lane

    def at(hop):
        return lax.rem(me + hop, slabs)

    def spread(body):
        lax.fori_loop(1, slabs, lambda hop, carry: (body(at(hop)), carry)[1], 0)

    barrier = pltpu.get_barrier_semaphore()

    def greet(dst):
        pl.semaphore_signal(barrier, inc=1, device_id=(lane, dst), device_id_type=MESH)

    spread(greet)
    pl.semaphore_signal(barrier, inc=1, device_id=(other, me), device_id_type=MESH)
    loads = [
        pltpu.make_async_copy(green_any, green, load_sem.at[0]),
        pltpu.make_async_copy(start_any.at[me], start, load_sem.at[1]),
        pltpu.make_async_copy(incident_any, inc, load_sem.at[2]),
    ]
    for load in loads:
        load.start()

    def remote(src, dst, send, recv, who):
        return pltpu.make_async_remote_copy(
            src_ref=src, dst_ref=dst, send_sem=send, recv_sem=recv,
            device_id=who, device_id_type=MESH,
        )

    def forward(plane, carry):
        c = contrast[plane]
        pair = jnp.concatenate([c * field[0, 0, plane], c * field[0, 1, plane]], axis=1)
        pair = transform_cols(pair, yfh, yfl)
        pair = transform_rows(pair, xh, xl, -1.0)
        out1[:, plane] = pair.reshape(slabs, cols_x, pair_y)
        return carry

    groups = math.gcd(local_depth, 2)
    size = local_depth // groups
    for group in range(groups):
        lax.fori_loop(group * size, (group + 1) * size, forward, 0)
        if group == 0:
            pl.semaphore_wait(barrier, slabs)
        part = pl.ds(group * size, size)
        spread(
            lambda dst: remote(
                out1.at[dst, part], in1.at[me, part], s1.at[dst], r1.at[me], (lane, dst)
            ).start()
        )
    in1[me] = out1[me]

    loads[0].wait()
    loads[1].wait()
    loads[2].wait()
    for first in range(0, cols_x, 8):
        rows = slice(first, first + 8)
        for half in range(2):
            cols = slice(half * width_y, (half + 1) * width_y)
            gbuf[rows, :, cols] = jnp.transpose(green[half, :, rows, :], (1, 0, 2))

    def arrived(src):
        remote(out1.at[src], in1.at[src], s1.at[src], r1.at[src], (lane, src)).wait_recv()

    spread(arrived)
    own = pl.ds(pl.multiple_of(me * cols_x, cols_x), cols_x)
    step_r, step_i = step_ref[own, :width_y], step_ref[own, width_y:]

    def horner(src, carry):
        real, imag = carry
        for plane in range(local_depth):
            real = real + in1[src, plane, :, :width_y]
            imag = imag + in1[src, plane, :, width_y:]
            real, imag = (real * step_r - imag * step_i, real * step_i + imag * step_r)
        return real, imag

    zero = jnp.zeros((cols_x, width_y), jnp.float32)
    real, imag = lax.fori_loop(0, slabs, horner, (zero, zero))
    real = real / root_depth - detector[0, 0]
    imag = imag / root_depth - detector[0, 1]
    misfit_out[0, 0] = real
    misfit_out[0, 1] = imag
    miss[me, :, :width_y] = real
    miss[me, :, width_y:] = imag
    spread(
        lambda dst: remote(miss.at[me], miss.at[me], sm.at[dst], rm.at[me], (lane, dst)).start()
    )

    for first in range(0, cols_x, 8):
        rows = slice(first, first + 8)
        block = in1[:, :, rows, :].reshape(depth, 8, pair_y)
        zbuf[rows] = jnp.transpose(block, (1, 0, 2))

    def convolve(row, carry):
        table = zt_ref[...]
        high, low = split_halves(zbuf[row])
        both = product(table, jnp.concatenate([high, low, high], axis=0))
        real, imag = combine(both, -1.0)
        g_real, g_imag = gbuf[row, :, :width_y], gbuf[row, :, width_y:]
        pair = jnp.concatenate(
            [g_real * real - g_imag * imag, g_real * imag + g_imag * real], axis=1
        )
        high, low = split_halves(pair)
        both = product(table, jnp.concatenate([high, low, high], axis=0))
        zbuf[row] = jnp.concatenate(combine(both, 1.0), axis=1)
        return carry

    lax.fori_loop(0, cols_x, convolve, 0)
    for first in range(0, cols_x, 8):
        rows = slice(first, first + 8)
        block = jnp.transpose(zbuf[rows], (1, 0, 2))
        out2[:, :, rows, :] = block.reshape(slabs, local_depth, 8, pair_y)
    spread(
        lambda dst: remote(out2.at[dst], in2.at[me], s2.at[dst], r2.at[me], (lane, dst)).start()
    )
    in2[me] = out2[me]

    spread(
        lambda src: remote(
            miss.at[src], miss.at[src], sm.at[src], rm.at[src], (lane, src)
        ).wait_recv()
    )
    gathered = miss[...].reshape(width_x, pair_y)
    m_real, m_imag = gathered[:, :width_y], gathered[:, width_y:]
    p_real, p_imag = start[:, :width_y], start[:, width_y:]
    rbuf[:, :width_y] = (p_real * m_real + p_imag * m_imag) / root_depth
    rbuf[:, width_y:] = (p_real * m_imag - p_imag * m_real) / root_depth

    def peer_copy(plane):
        return remote(
            gmine.at[plane], gpeer.at[plane], sg.at[plane], rg.at[plane], (other, me)
        )

    def project(count, carry):
        plane = local_depth - 1 - count
        now = rbuf[...]
        pair = transform_rows(now, xh, xl, 1.0)
        pair = transform_cols(pair, yih, yil)
        gmine[plane] = field[0, 0, plane] * pair[:, :width_y] + field[0, 1, plane] * pair[:, width_y:]
        peer_copy(plane).start()
        now_r, now_i = now[:, :width_y], now[:, width_y:]
        w_real, w_imag = step_ref[:, :width_y], step_ref[:, width_y:]
        rbuf[:, :width_y] = w_real * now_r + w_imag * now_i
        rbuf[:, width_y:] = w_real * now_i - w_imag * now_r
        return carry

    lax.fori_loop(0, local_depth, project, 0)

    def update(count, carry):
        plane = local_depth - 1 - count
        peer_copy(plane).wait()
        cube[passes + plane] = contrast[plane] - step_size * (gmine[plane] + gpeer[plane])
        return carry

    lax.fori_loop(0, local_depth, update, 0)
    low_side, high_side = pl.ds(0, passes), pl.ds(passes + local_depth, passes)
    up = remote(
        cube.at[pl.ds(local_depth, passes)], cube.at[low_side], sh.at[0], rh.at[0],
        (lane, lax.rem(me + 1, slabs)),
    )
    down = remote(
        cube.at[pl.ds(passes, passes)], cube.at[high_side], sh.at[1], rh.at[1],
        (lane, lax.rem(me + slabs - 1, slabs)),
    )
    has_up, has_down = me < slabs - 1, me > 0
    pl.when(has_up)(up.start)
    pl.when(has_down)(down.start)

    @pl.when(me == 0)
    def _():
        cube[low_side] = jnp.zeros((passes, width_x, width_y), jnp.float32)

    @pl.when(me == slabs - 1)
    def _():
        cube[high_side] = jnp.zeros((passes, width_x, width_y), jnp.float32)

    pl.when(has_up)(up.wait_send)
    pl.when(has_down)(down.wait_send)
    pl.when(has_down)(up.wait_recv)
    pl.when(has_up)(down.wait_recv)

    row_at = lax.broadcasted_iota(jnp.int32, (width_x, width_y), 0)
    col_at = lax.broadcasted_iota(jnp.int32, (width_x, width_y), 1)

    def sweep(source, plane, write):
        cur = source[plane]
        place = me * local_depth - passes + plane
        inside = jnp.where((place >= 0) & (place <= depth - 2), 1.0, 0.0)
        slope_z = (source[plane + 1] - cur) * inside
        flux_x = jnp.where(row_at < width_x - 1, pltpu.roll(cur, width_x - 1, 0) - cur, 0.0)
        flux_y = jnp.where(col_at < width_y - 1, pltpu.roll(cur, width_y - 1, 1) - cur, 0.0)
        scale = lax.rsqrt(slope_z**2 + flux_x**2 + flux_y**2 + edge_scale**2)
        flux_z = slope_z * scale
        if write is not None:
            flux_x = flux_x * scale
            flux_y = flux_y * scale
            total = flux_z - fz[...] + flux_x - pltpu.roll(flux_x, 1, 0)
            total = total + flux_y - pltpu.roll(flux_y, 1, 1)
            write(plane, cur + diffusion * total)
        fz[...] = flux_z

    planes = local_depth + 2 * passes
    for turn in range(passes):
        source, target = (cube, cube2) if turn % 2 == 0 else (cube2, cube)
        sweep(source, turn, None)

        def write(plane, value, turn=turn, target=target):
            if turn == passes - 1:
                contrast_out[plane - passes] = value
            else:
                target[plane] = value

        def one(plane, carry, source=source, write=write):
            sweep(source, plane, write)
            return carry

        lax.fori_loop(turn + 1, planes - 1 - turn, one, 0)

    spread(
        lambda src: remote(
            out2.at[src], in2.at[src], s2.at[src], r2.at[src], (lane, src)
        ).wait_recv()
    )

    def finish(plane, carry):
        pair = in2[:, plane].reshape(width_x, pair_y)
        pair = transform_rows(pair, xh, xl, 1.0)
        pair = transform_cols(pair, yih, yil)
        field_out[0, 0, plane] = inc[0, 0, plane].astype(jnp.float32) + pair[:, :width_y]
        field_out[0, 1, plane] = inc[0, 1, plane].astype(jnp.float32) + pair[:, width_y:]
        return carry

    lax.fori_loop(0, local_depth, finish, 0)

    def drain(dst):
        remote(out1.at[dst], in1.at[me], s1.at[dst], r1.at[me], (lane, dst)).wait_send()
        remote(miss.at[me], miss.at[me], sm.at[dst], rm.at[me], (lane, dst)).wait_send()
        remote(out2.at[dst], in2.at[me], s2.at[dst], r2.at[me], (lane, dst)).wait_send()

    spread(drain)


def fused(incident, field_now, contrast, green_spectrum, detector_data):
    slabs = lax.axis_size("slab")
    local_depth, width_x, width_y = contrast.shape
    depth = local_depth * slabs
    cols_x = width_x // slabs
    pair_y = 2 * width_y
    cos_x, sin_x = host_tables(width_x)
    cos_y, sin_y = host_tables(width_y)
    cos_z, sin_z = host_tables(depth)
    xh, xl = host_split(np.concatenate([cos_x, sin_x], axis=0))
    yfh, yfl = host_split(np.block([[cos_y, -sin_y], [sin_y, cos_y]]))
    yih, yil = host_split(np.block([[cos_y, sin_y], [-sin_y, cos_y]]))
    zh, zl = host_split(np.concatenate([cos_z, sin_z], axis=0))
    zt = np.concatenate([zh, zh, zl], axis=1)
    step = host_propagator(1, width_x, width_y)
    nearest = [depth - (s * local_depth + local_depth - 1) for s in range(slabs)]
    start = np.stack([host_propagator(d, width_x, width_y) for d in nearest])
    vmem, anywhere = pl.BlockSpec(memory_space=pltpu.VMEM), pl.BlockSpec(memory_space=pl.ANY)
    f32 = jnp.float32
    block = pltpu.VMEM((slabs, local_depth, cols_x, pair_y), f32)
    planes = pltpu.VMEM((local_depth, width_x, width_y), f32)
    padded = pltpu.VMEM((local_depth + 2 * passes, width_x, width_y), f32)
    turned = pltpu.VMEM((cols_x, depth, pair_y), f32)
    several = pltpu.SemaphoreType.DMA((slabs,))
    return pl.pallas_call(
        fused_kernel,
        out_shape=(
            jax.ShapeDtypeStruct(field_now.shape, f32),
            jax.ShapeDtypeStruct(detector_data.shape, f32),
            jax.ShapeDtypeStruct(contrast.shape, f32),
        ),
        in_specs=[vmem] * 11 + [anywhere] * 3,
        out_specs=(vmem, vmem, vmem),
        scratch_shapes=[
            block, block, block, block,
            pltpu.VMEM((slabs, cols_x, pair_y), f32),
            planes, planes, padded, padded, turned, turned,
            pltpu.VMEM((width_x, pair_y), f32),
            pltpu.VMEM((width_x, width_y), f32),
            pltpu.VMEM(incident.shape, jnp.bfloat16),
            pltpu.VMEM(green_spectrum.shape, f32),
            pltpu.VMEM((width_x, pair_y), f32),
            pltpu.SemaphoreType.DMA((3,)),
            several, several, several, several, several, several,
            pltpu.SemaphoreType.DMA((local_depth,)),
            pltpu.SemaphoreType.DMA((local_depth,)),
            pltpu.SemaphoreType.DMA((2,)),
            pltpu.SemaphoreType.DMA((2,)),
        ],
        compiler_params=pltpu.CompilerParams(
            collective_id=0, has_side_effects=True, vmem_limit_bytes=48 * 2**20
        ),
    )(
        field_now, contrast, detector_data, xh, xl, yfh, yfl, yih, yil, zt, step,
        incident, green_spectrum, start,
    )


def whole_tiles(mesh, arrays):
    local_depth = arrays[2].shape[0]
    rows = arrays[3].shape[2]
    return (
        mesh.shape["illum"] == 2
        and mesh.shape["slab"] > 1
        and rows % 8 == 0
        and (local_depth * mesh.shape["slab"]) % 16 == 0
        and arrays[2].shape[2] % 128 == 0
        and local_depth >= passes
    )


def solution(mesh):
    placed = (
        P("illum", None, "slab", None, None),
        P("illum", None, "slab", None, None),
        P("slab", None, None),
        P(None, None, "slab", None),
        P("illum", None, "slab", None),
    )

    def pick(*arrays):
        return (fused if whole_tiles(mesh, arrays) else shards)(*arrays)

    return jax.shard_map(
        pick,
        mesh=mesh,
        in_specs=placed,
        out_specs=(
            P("illum", None, "slab", None, None),
            P("illum", None, "slab", None),
            P("slab", None, None),
        ),
        check_vma=False,
    )
```

```python
import math

import jax
import jax.numpy as jnp
import numpy as np
from jax import lax
from jax.experimental import pallas as pl
from jax.experimental.pallas import tpu as pltpu
from jax.sharding import PartitionSpec as P

wave_number = 1.2
step_size = 2.0
diffusion = 0.02
edge_scale = 0.25
passes = 4
MESH = pl.DeviceIdType.MESH
highest = lax.Precision.HIGH
form_rows = "...xy,xk->...ky"
form_cols = "...y,yk->...k"
form_depth = "azxy,zk->akxy"


def with_halo(array, sides, width):
    for axis, dim in sides:
        devices, length = (lax.axis_size(axis), array.shape[dim])
        up = [(i, (i + 1) % devices) for i in range(devices - 1)]
        down = [(j, i) for i, j in up]
        last = lax.slice_in_dim(array, length - width, length, axis=dim)
        leading = lax.slice_in_dim(array, 0, width, axis=dim)
        before = lax.ppermute(last, axis, up)
        after = lax.ppermute(leading, axis, down)
        array = jnp.concatenate([before, array, after], axis=dim)
    return array


def tables(length):
    counter = jnp.arange(length, dtype=jnp.int32)
    product = counter[:, None] * counter[None, :] % length
    angle = product.astype(jnp.float32) * (2.0 * math.pi / length)
    scale = 1.0 / math.sqrt(length)
    return (jnp.cos(angle) * scale, jnp.sin(angle) * scale)


def mixing(real, imag, cosine, sine_table, sign, form):
    real_cos = jnp.einsum(form, real, cosine, precision=highest)
    real_sin = jnp.einsum(form, real, sine_table, precision=highest)
    imag_cos = jnp.einsum(form, imag, cosine, precision=highest)
    imag_sin = jnp.einsum(form, imag, sine_table, precision=highest)
    return (real_cos - sign * imag_sin, imag_cos + sign * real_sin)


def frequency(index, length):
    shifted = jnp.where(index < length // 2, index, index - length)
    return shifted.astype(jnp.float32) * (2.0 * math.pi / length)


def propagator(depth_index, row_index, width_x, width_y, depth):
    along_x = frequency(row_index, width_x)
    along_y = frequency(jnp.arange(width_y, dtype=jnp.int32), width_y)
    squared = wave_number**2 - along_x[None, :, None] ** 2 - along_y[None, None, :] ** 2
    distance = (depth - depth_index).astype(jnp.float32)[:, None, None]
    root = jnp.sqrt(jnp.abs(squared))
    moving = squared > 0.0
    amplitude = jnp.where(moving, 1.0, jnp.exp(-root * distance))
    phase = jnp.where(moving, root * distance, 0.0)
    return (amplitude * jnp.cos(phase), amplitude * jnp.sin(phase))


def tv_pass(padded, first, depth):
    rows = padded.shape[0]
    global_row = first + jnp.arange(rows - 1, dtype=jnp.int32)
    inside = (global_row >= 0) & (global_row <= depth - 2)
    core = padded[:-1]
    slope_depth = jnp.where(inside[:, None, None], padded[1:] - core, 0.0)
    slope_rows = jnp.concatenate([core[:, 1:] - core[:, :-1], jnp.zeros_like(core[:, :1])], axis=1)
    slope_cols = jnp.concatenate(
        [core[:, :, 1:] - core[:, :, :-1], jnp.zeros_like(core[:, :, :1])], axis=2
    )
    magnitude = jnp.sqrt(slope_depth**2 + slope_rows**2 + slope_cols**2 + edge_scale**2)
    flux_depth = slope_depth / magnitude
    flux_rows = (slope_rows / magnitude)[1:]
    flux_cols = (slope_cols / magnitude)[1:]
    spread_depth = flux_depth[1:] - flux_depth[:-1]
    spread_rows = flux_rows - jnp.concatenate(
        [jnp.zeros_like(flux_rows[:, :1]), flux_rows[:, :-1]], axis=1
    )
    spread_cols = flux_cols - jnp.concatenate(
        [jnp.zeros_like(flux_cols[:, :, :1]), flux_cols[:, :, :-1]], axis=2
    )
    return padded[1:-1] + diffusion * (spread_depth + spread_rows + spread_cols)


def back_project(prop_real, prop_imag, mismatch, root_depth):
    miss_real = mismatch[:, 0][:, None]
    miss_imag = mismatch[:, 1][:, None]
    out_real = (prop_real[None] * miss_real + prop_imag[None] * miss_imag) / root_depth
    out_imag = (prop_real[None] * miss_imag - prop_imag[None] * miss_real) / root_depth
    return jnp.stack([out_real, out_imag], 1)


def shards(incident, field_now, contrast, green_spectrum, detector_data):
    slabs = lax.axis_size("slab")
    place = lax.axis_index("slab")
    local_depth, width_x, width_y = contrast.shape
    depth = local_depth * slabs
    cols_x = width_x // slabs
    root_depth = math.sqrt(depth)
    cos_x, sin_x = tables(width_x)
    cos_y, sin_y = tables(width_y)
    cos_z, sin_z = tables(depth)
    real_now = field_now[:, 0]
    imag_now = field_now[:, 1]
    spec_real, spec_imag = mixing(
        contrast[None] * real_now, contrast[None] * imag_now, cos_x, sin_x, -1.0, form_rows
    )
    spec_real, spec_imag = mixing(spec_real, spec_imag, cos_y, sin_y, -1.0, form_cols)
    spectrum = jnp.stack([spec_real, spec_imag], 1)
    columns = lax.all_to_all(spectrum, "slab", split_axis=3, concat_axis=2, tiled=True)
    deep_real, deep_imag = mixing(columns[:, 0], columns[:, 1], cos_z, sin_z, -1.0, form_depth)
    green_real = green_spectrum[0][None]
    green_imag = green_spectrum[1][None]
    prod_real = green_real * deep_real - green_imag * deep_imag
    prod_imag = green_real * deep_imag + green_imag * deep_real
    vol_real, vol_imag = mixing(prod_real, prod_imag, cos_z, sin_z, 1.0, form_depth)
    volume = jnp.stack([vol_real, vol_imag], 1)
    kx_index = place * cols_x + jnp.arange(cols_x, dtype=jnp.int32)
    col_prop_real, col_prop_imag = propagator(
        jnp.arange(depth, dtype=jnp.int32), kx_index, width_x, width_y, depth
    )
    col_real = columns[:, 0]
    col_imag = columns[:, 1]
    pred_real = (
        jnp.sum(col_prop_real[None] * col_real - col_prop_imag[None] * col_imag, axis=1)
        / root_depth
    )
    pred_imag = (
        jnp.sum(col_prop_real[None] * col_imag + col_prop_imag[None] * col_real, axis=1)
        / root_depth
    )
    mismatch = jnp.stack([pred_real, pred_imag], 1) - detector_data
    volume = lax.all_to_all(volume, "slab", split_axis=2, concat_axis=3, tiled=True)
    depth_index = place * local_depth + jnp.arange(local_depth, dtype=jnp.int32)
    prop_real, prop_imag = propagator(
        depth_index, jnp.arange(width_x, dtype=jnp.int32), width_x, width_y, depth
    )
    gathered = lax.all_gather(mismatch, "slab", axis=2, tiled=True)
    returned = back_project(prop_real, prop_imag, gathered, root_depth)
    scat_real, scat_imag = mixing(volume[:, 0], volume[:, 1], cos_x, sin_x, 1.0, form_rows)
    scat_real, scat_imag = mixing(scat_real, scat_imag, cos_y, sin_y, 1.0, form_cols)
    field_next = incident.astype(jnp.float32) + jnp.stack([scat_real, scat_imag], 1)
    ret_real, ret_imag = mixing(returned[:, 0], returned[:, 1], cos_x, sin_x, 1.0, form_rows)
    ret_real, ret_imag = mixing(ret_real, ret_imag, cos_y, sin_y, 1.0, form_cols)
    local_terms = jnp.sum(real_now * ret_real + imag_now * ret_imag, axis=0)
    illums = lax.axis_size("illum")
    gradient, travelling = local_terms, local_terms
    for hop in range(illums - 1):
        travelling = lax.ppermute(travelling, "illum", [(i, (i + 1) % illums) for i in range(illums)])
        gradient = gradient + travelling
    updated = contrast - step_size * gradient
    wide = math.gcd(passes, local_depth)
    for repeat in range(passes // wide):
        updated = with_halo(updated, (("slab", 0),), wide)
        for left in range(wide, 0, -1):
            updated = tv_pass(updated, place * local_depth - left, depth)
    return (field_next, mismatch, updated)


def split_halves(value):
    high = value.astype(jnp.bfloat16)
    return high, (value - high.astype(jnp.float32)).astype(jnp.bfloat16)


def product(left, right):
    return jnp.dot(left, right, preferred_element_type=jnp.float32)


def combine(both, sign):
    rows, cols = both.shape[0] // 2, both.shape[1] // 2
    by_cos, by_sin = both[:rows], both[rows:]
    real = by_cos[:, :cols] - sign * by_sin[:, cols:]
    imag = by_cos[:, cols:] + sign * by_sin[:, :cols]
    return real, imag


def transform_rows(pair, high_ref, low_ref, sign):
    high, low = split_halves(pair)
    table = high_ref[...]
    both = product(table, high) + product(table, low) + product(low_ref[...], high)
    return jnp.concatenate(combine(both, sign), axis=1)


def transform_cols(pair, high_ref, low_ref):
    high, low = split_halves(pair)
    table = high_ref[...]
    return product(high, table) + product(low, table) + product(high, low_ref[...])


def host_tables(length):
    counter = np.arange(length)
    angle = (counter[:, None] * counter[None, :] % length) * (2.0 * math.pi / length)
    return np.cos(angle) / math.sqrt(length), np.sin(angle) / math.sqrt(length)


def host_frequency(length):
    index = np.arange(length)
    return np.where(index < length // 2, index, index - length) * (2.0 * math.pi / length)


def host_propagator(distance, width_x, width_y):
    squared = (
        wave_number**2 - host_frequency(width_x)[:, None] ** 2 - host_frequency(width_y)[None] ** 2
    )
    root = np.sqrt(np.abs(squared))
    moving = squared > 0.0
    amplitude = np.where(moving, 1.0, np.exp(-root * distance))
    phase = np.where(moving, root * distance, 0.0)
    pair = [amplitude * np.cos(phase), amplitude * np.sin(phase)]
    return np.concatenate(pair, axis=1).astype(np.float32)


def fused_kernel(
    field_any, contrast_any, yf_any, x_any, green_any, step_any,
    detector_any, z_any, start_any, yi_any, incident_any,
    field_out, misfit_out, contrast_out,
    out1, in1, out2, in2, miss, gmine, gpeer, cube, cube2, zbuf, gbuf, rbuf, fz,
    field, contrast, yf, xt, green, step_ref, detector, zf, start, yi, inc,
    yfh, yfl, yih, yil, xh, xl, zt_ref,
    load_sem, s1, r1, s2, r2, sm, rm, sg, rg, sh, rh,
):
    slabs, local_depth, cols_x, pair_y = out1.shape
    width_y = pair_y // 2
    width_x = slabs * cols_x
    depth = slabs * local_depth
    root_depth = math.sqrt(depth)
    me = lax.axis_index("slab")
    lane = lax.axis_index("illum")
    other = 1 - lane

    def at(hop):
        return lax.rem(me + hop, slabs)

    def spread(body):
        lax.fori_loop(1, slabs, lambda hop, carry: (body(at(hop)), carry)[1], 0)

    barrier = pltpu.get_barrier_semaphore()

    def greet(dst):
        pl.semaphore_signal(barrier, inc=1, device_id=(lane, dst), device_id_type=MESH)

    sources = [
        field_any, contrast_any, yf_any, x_any, green_any, step_any,
        detector_any, z_any, start_any.at[me], yi_any, incident_any,
    ]
    held = [field, contrast, yf, xt, green, step_ref, detector, zf, start, yi, inc]
    early = 4
    loads = [
        pltpu.make_async_copy(src, dst, load_sem.at[i])
        for i, (src, dst) in enumerate(zip(sources, held))
    ]
    for load in loads:
        load.start()
    spread(greet)
    pl.semaphore_signal(barrier, inc=1, device_id=(other, me), device_id_type=MESH)

    def remote(src, dst, send, recv, who):
        return pltpu.make_async_remote_copy(
            src_ref=src, dst_ref=dst, send_sem=send, recv_sem=recv,
            device_id=who, device_id_type=MESH,
        )

    def forward(plane, carry):
        c = contrast[plane]
        pair = jnp.concatenate([c * field[0, 0, plane], c * field[0, 1, plane]], axis=1)
        pair = transform_cols(pair, yfh, yfl)
        pair = transform_rows(pair, xh, xl, -1.0)
        out1[:, plane] = pair.reshape(slabs, cols_x, pair_y)
        return carry

    for load in loads[:early]:
        load.wait()
    yfh[...], yfl[...] = split_halves(yf[...])
    xh[...], xl[...] = split_halves(xt[...])
    parts = cols_x // 8
    groups = math.gcd(local_depth, 2)
    size = local_depth // groups

    def send_block(part, first, count):
        planes, rows = pl.ds(first, count), pl.ds(part * 8, 8)
        spread(
            lambda dst: remote(
                out1.at[dst, planes, rows], in1.at[me, planes, rows],
                s1.at[part, dst], r1.at[part, me], (lane, dst),
            ).start()
        )

    for group in range(groups):
        lax.fori_loop(group * size, (group + 1) * size, forward, 0)
        if group == 0:
            pl.semaphore_wait(barrier, slabs)
        send_block(0, group * size, size)
    for part in range(1, parts):
        send_block(part, 0, local_depth)
    in1[me] = out1[me]

    for load in loads[early:]:
        load.wait()
    yih[...], yil[...] = split_halves(yi[...])
    z_high, z_low = split_halves(zf[...])
    zt_ref[...] = jnp.concatenate([z_high, z_high, z_low, z_low], axis=1)
    for first in range(0, cols_x, 8):
        rows = slice(first, first + 8)
        for half in range(2):
            cols = slice(half * width_y, (half + 1) * width_y)
            gbuf[rows, :, cols] = jnp.transpose(green[half, :, rows, :], (1, 0, 2))

    def convolve(row, carry):
        table = zt_ref[...]
        high, low = split_halves(zbuf[row])
        both = product(table, jnp.concatenate([high, low, high, low], axis=0))
        real, imag = combine(both, -1.0)
        g_real, g_imag = gbuf[row, :, :width_y], gbuf[row, :, width_y:]
        pair = jnp.concatenate(
            [g_real * real - g_imag * imag, g_real * imag + g_imag * real], axis=1
        )
        high, low = split_halves(pair)
        both = product(table, jnp.concatenate([high, low, high, low], axis=0))
        zbuf[row] = jnp.concatenate(combine(both, 1.0), axis=1)
        return carry

    for part in range(parts):
        rows, cut = slice(part * 8, part * 8 + 8), pl.ds(part * 8, 8)
        spread(
            lambda src: remote(
                out1.at[src, :, cut], in1.at[src, :, cut],
                s1.at[part, src], r1.at[part, src], (lane, src),
            ).wait_recv()
        )
        own = pl.ds(pl.multiple_of(me * cols_x + part * 8, 8), 8)
        step_r, step_i = step_ref[own, :width_y], step_ref[own, width_y:]

        def horner(src, carry):
            real, imag = carry
            for plane in range(local_depth):
                real = real + in1[src, plane, rows, :width_y]
                imag = imag + in1[src, plane, rows, width_y:]
                real, imag = (real * step_r - imag * step_i, real * step_i + imag * step_r)
            return real, imag

        zero = jnp.zeros((8, width_y), jnp.float32)
        real, imag = lax.fori_loop(0, slabs, horner, (zero, zero))
        real = real / root_depth - detector[0, 0, rows]
        imag = imag / root_depth - detector[0, 1, rows]
        misfit_out[0, 0, rows] = real
        misfit_out[0, 1, rows] = imag
        miss[me, rows, :width_y] = real
        miss[me, rows, width_y:] = imag
        spread(
            lambda dst: remote(
                miss.at[me, cut], miss.at[me, cut],
                sm.at[part, dst], rm.at[part, me], (lane, dst),
            ).start()
        )
        block = in1[:, :, rows, :].reshape(depth, 8, pair_y)
        zbuf[rows] = jnp.transpose(block, (1, 0, 2))
        lax.fori_loop(part * 8, part * 8 + 8, convolve, 0)
        block = jnp.transpose(zbuf[rows], (1, 0, 2))
        out2[:, :, rows, :] = block.reshape(slabs, local_depth, 8, pair_y)
        spread(
            lambda dst: remote(
                out2.at[dst, :, cut], in2.at[me, :, cut],
                s2.at[part, dst], r2.at[part, me], (lane, dst),
            ).start()
        )
    in2[me] = out2[me]

    for part in range(parts):
        cut = pl.ds(part * 8, 8)
        spread(
            lambda src: remote(
                miss.at[src, cut], miss.at[src, cut],
                sm.at[part, src], rm.at[part, src], (lane, src),
            ).wait_recv()
        )
    gathered = miss[...].reshape(width_x, pair_y)
    m_real, m_imag = gathered[:, :width_y], gathered[:, width_y:]
    p_real, p_imag = start[:, :width_y], start[:, width_y:]
    rbuf[:, :width_y] = (p_real * m_real + p_imag * m_imag) / root_depth
    rbuf[:, width_y:] = (p_real * m_imag - p_imag * m_real) / root_depth

    def peer_copy(plane):
        return remote(
            gmine.at[plane], gpeer.at[plane], sg.at[plane], rg.at[plane], (other, me)
        )

    def project(count, carry):
        plane = local_depth - 1 - count
        now = rbuf[...]
        pair = transform_rows(now, xh, xl, 1.0)
        pair = transform_cols(pair, yih, yil)
        gmine[plane] = field[0, 0, plane] * pair[:, :width_y] + field[0, 1, plane] * pair[:, width_y:]
        peer_copy(plane).start()
        now_r, now_i = now[:, :width_y], now[:, width_y:]
        w_real, w_imag = step_ref[:, :width_y], step_ref[:, width_y:]
        rbuf[:, :width_y] = w_real * now_r + w_imag * now_i
        rbuf[:, width_y:] = w_real * now_i - w_imag * now_r
        return carry

    lax.fori_loop(0, local_depth, project, 0)

    def update(count, carry):
        plane = local_depth - 1 - count
        peer_copy(plane).wait()
        cube[passes + plane] = contrast[plane] - step_size * (gmine[plane] + gpeer[plane])
        return carry

    lax.fori_loop(0, local_depth, update, 0)
    low_side, high_side = pl.ds(0, passes), pl.ds(passes + local_depth, passes)
    up = remote(
        cube.at[pl.ds(local_depth, passes)], cube.at[low_side], sh.at[0], rh.at[0],
        (lane, lax.rem(me + 1, slabs)),
    )
    down = remote(
        cube.at[pl.ds(passes, passes)], cube.at[high_side], sh.at[1], rh.at[1],
        (lane, lax.rem(me + slabs - 1, slabs)),
    )
    has_up, has_down = me < slabs - 1, me > 0
    pl.when(has_up)(up.start)
    pl.when(has_down)(down.start)

    @pl.when(me == 0)
    def _():
        cube[low_side] = jnp.zeros((passes, width_x, width_y), jnp.float32)

    @pl.when(me == slabs - 1)
    def _():
        cube[high_side] = jnp.zeros((passes, width_x, width_y), jnp.float32)

    pl.when(has_up)(up.wait_send)
    pl.when(has_down)(down.wait_send)
    pl.when(has_down)(up.wait_recv)
    pl.when(has_up)(down.wait_recv)

    row_at = lax.broadcasted_iota(jnp.int32, (width_x, width_y), 0)
    col_at = lax.broadcasted_iota(jnp.int32, (width_x, width_y), 1)

    def sweep(source, plane, write):
        cur = source[plane]
        place = me * local_depth - passes + plane
        inside = jnp.where((place >= 0) & (place <= depth - 2), 1.0, 0.0)
        slope_z = (source[plane + 1] - cur) * inside
        flux_x = jnp.where(row_at < width_x - 1, pltpu.roll(cur, width_x - 1, 0) - cur, 0.0)
        flux_y = jnp.where(col_at < width_y - 1, pltpu.roll(cur, width_y - 1, 1) - cur, 0.0)
        scale = lax.rsqrt(slope_z**2 + flux_x**2 + flux_y**2 + edge_scale**2)
        flux_z = slope_z * scale
        if write is not None:
            flux_x = flux_x * scale
            flux_y = flux_y * scale
            total = flux_z - fz[...] + flux_x - pltpu.roll(flux_x, 1, 0)
            total = total + flux_y - pltpu.roll(flux_y, 1, 1)
            write(plane, cur + diffusion * total)
        fz[...] = flux_z

    planes = local_depth + 2 * passes
    for turn in range(passes):
        source, target = (cube, cube2) if turn % 2 == 0 else (cube2, cube)
        sweep(source, turn, None)

        def write(plane, value, turn=turn, target=target):
            if turn == passes - 1:
                contrast_out[plane - passes] = value
            else:
                target[plane] = value

        def one(plane, carry, source=source, write=write):
            sweep(source, plane, write)
            return carry

        lax.fori_loop(turn + 1, planes - 1 - turn, one, 0)

    for part in range(parts):
        cut = pl.ds(part * 8, 8)
        spread(
            lambda src: remote(
                out2.at[src, :, cut], in2.at[src, :, cut],
                s2.at[part, src], r2.at[part, src], (lane, src),
            ).wait_recv()
        )

    def finish(plane, carry):
        pair = in2[:, plane].reshape(width_x, pair_y)
        pair = transform_rows(pair, xh, xl, 1.0)
        pair = transform_cols(pair, yih, yil)
        field_out[0, 0, plane] = inc[0, 0, plane].astype(jnp.float32) + pair[:, :width_y]
        field_out[0, 1, plane] = inc[0, 1, plane].astype(jnp.float32) + pair[:, width_y:]
        return carry

    lax.fori_loop(0, local_depth, finish, 0)

    def drain(part, dst):
        cut = pl.ds(part * 8, 8)
        who = (lane, dst)
        remote(
            out1.at[dst, :, cut], in1.at[me, :, cut], s1.at[part, dst], r1.at[part, me], who
        ).wait_send()
        remote(
            miss.at[me, cut], miss.at[me, cut], sm.at[part, dst], rm.at[part, me], who
        ).wait_send()
        remote(
            out2.at[dst, :, cut], in2.at[me, :, cut], s2.at[part, dst], r2.at[part, me], who
        ).wait_send()

    for part in range(parts):
        spread(lambda dst: drain(part, dst))


def fused(incident, field_now, contrast, green_spectrum, detector_data):
    slabs = lax.axis_size("slab")
    local_depth, width_x, width_y = contrast.shape
    depth = local_depth * slabs
    cols_x = width_x // slabs
    pair_y = 2 * width_y
    cos_x, sin_x = host_tables(width_x)
    cos_y, sin_y = host_tables(width_y)
    cos_z, sin_z = host_tables(depth)
    table_x = np.concatenate([cos_x, sin_x], axis=0).astype(np.float32)
    forward_y = np.block([[cos_y, -sin_y], [sin_y, cos_y]]).astype(np.float32)
    inverse_y = np.block([[cos_y, sin_y], [-sin_y, cos_y]]).astype(np.float32)
    table_z = np.concatenate([cos_z, sin_z], axis=0).astype(np.float32)
    step = host_propagator(1, width_x, width_y)
    nearest = [depth - (s * local_depth + local_depth - 1) for s in range(slabs)]
    start = np.stack([host_propagator(d, width_x, width_y) for d in nearest])
    vmem, anywhere = pl.BlockSpec(memory_space=pltpu.VMEM), pl.BlockSpec(memory_space=pl.ANY)
    f32 = jnp.float32
    block = pltpu.VMEM((slabs, local_depth, cols_x, pair_y), f32)
    planes = pltpu.VMEM((local_depth, width_x, width_y), f32)
    padded = pltpu.VMEM((local_depth + 2 * passes, width_x, width_y), f32)
    turned = pltpu.VMEM((cols_x, depth, pair_y), f32)
    cols_table = pltpu.VMEM((pair_y, pair_y), jnp.bfloat16)
    rows_table = pltpu.VMEM((2 * width_x, width_x), jnp.bfloat16)
    several = pltpu.SemaphoreType.DMA((cols_x // 8, slabs))
    return pl.pallas_call(
        fused_kernel,
        out_shape=(
            jax.ShapeDtypeStruct(field_now.shape, f32),
            jax.ShapeDtypeStruct(detector_data.shape, f32),
            jax.ShapeDtypeStruct(contrast.shape, f32),
        ),
        in_specs=[anywhere] * 11,
        out_specs=(vmem, vmem, vmem),
        scratch_shapes=[
            block, block, block, block,
            pltpu.VMEM((slabs, cols_x, pair_y), f32),
            planes, planes, padded, padded, turned, turned,
            pltpu.VMEM((width_x, pair_y), f32),
            pltpu.VMEM((width_x, width_y), f32),
            pltpu.VMEM(field_now.shape, f32),
            planes,
            pltpu.VMEM(forward_y.shape, f32),
            pltpu.VMEM(table_x.shape, f32),
            pltpu.VMEM(green_spectrum.shape, f32),
            pltpu.VMEM((width_x, pair_y), f32),
            pltpu.VMEM(detector_data.shape, f32),
            pltpu.VMEM(table_z.shape, f32),
            pltpu.VMEM((width_x, pair_y), f32),
            pltpu.VMEM(inverse_y.shape, f32),
            pltpu.VMEM(incident.shape, jnp.bfloat16),
            cols_table, cols_table, cols_table, cols_table, rows_table, rows_table,
            pltpu.VMEM((2 * depth, 4 * depth), jnp.bfloat16),
            pltpu.SemaphoreType.DMA((11,)),
            several, several, several, several, several, several,
            pltpu.SemaphoreType.DMA((local_depth,)),
            pltpu.SemaphoreType.DMA((local_depth,)),
            pltpu.SemaphoreType.DMA((2,)),
            pltpu.SemaphoreType.DMA((2,)),
        ],
        compiler_params=pltpu.CompilerParams(
            collective_id=0, has_side_effects=True, vmem_limit_bytes=60 * 2**20
        ),
    )(
        field_now, contrast, forward_y, table_x, green_spectrum, step,
        detector_data, table_z, start, inverse_y, incident,
    )


def whole_tiles(mesh, arrays):
    local_depth = arrays[2].shape[0]
    rows = arrays[3].shape[2]
    return (
        mesh.shape["illum"] == 2
        and mesh.shape["slab"] > 1
        and rows % 8 == 0
        and (local_depth * mesh.shape["slab"]) % 16 == 0
        and arrays[2].shape[2] % 128 == 0
        and local_depth >= passes
    )


def solution(mesh):
    placed = (
        P("illum", None, "slab", None, None),
        P("illum", None, "slab", None, None),
        P("slab", None, None),
        P(None, None, "slab", None),
        P("illum", None, "slab", None),
    )

    def pick(*arrays):
        return (fused if whole_tiles(mesh, arrays) else shards)(*arrays)

    return jax.shard_map(
        pick,
        mesh=mesh,
        in_specs=placed,
        out_specs=(
            P("illum", None, "slab", None, None),
            P("illum", None, "slab", None),
            P("slab", None, None),
        ),
        check_vma=False,
    )
```

```python
import math

import jax
import jax.numpy as jnp
import numpy as np
from jax import lax
from jax.experimental import pallas as pl
from jax.experimental.pallas import tpu as pltpu
from jax.sharding import PartitionSpec as P

wave_number = 1.2
step_size = 2.0
diffusion = 0.02
edge_scale = 0.25
passes = 4
MESH = pl.DeviceIdType.MESH
highest = lax.Precision.HIGH
form_rows = "...xy,xk->...ky"
form_cols = "...y,yk->...k"
form_depth = "azxy,zk->akxy"


def with_halo(array, sides, width):
    for axis, dim in sides:
        devices, length = (lax.axis_size(axis), array.shape[dim])
        up = [(i, (i + 1) % devices) for i in range(devices - 1)]
        down = [(j, i) for i, j in up]
        last = lax.slice_in_dim(array, length - width, length, axis=dim)
        leading = lax.slice_in_dim(array, 0, width, axis=dim)
        before = lax.ppermute(last, axis, up)
        after = lax.ppermute(leading, axis, down)
        array = jnp.concatenate([before, array, after], axis=dim)
    return array


def tables(length):
    counter = jnp.arange(length, dtype=jnp.int32)
    product = counter[:, None] * counter[None, :] % length
    angle = product.astype(jnp.float32) * (2.0 * math.pi / length)
    scale = 1.0 / math.sqrt(length)
    return (jnp.cos(angle) * scale, jnp.sin(angle) * scale)


def mixing(real, imag, cosine, sine_table, sign, form):
    real_cos = jnp.einsum(form, real, cosine, precision=highest)
    real_sin = jnp.einsum(form, real, sine_table, precision=highest)
    imag_cos = jnp.einsum(form, imag, cosine, precision=highest)
    imag_sin = jnp.einsum(form, imag, sine_table, precision=highest)
    return (real_cos - sign * imag_sin, imag_cos + sign * real_sin)


def frequency(index, length):
    shifted = jnp.where(index < length // 2, index, index - length)
    return shifted.astype(jnp.float32) * (2.0 * math.pi / length)


def propagator(depth_index, row_index, width_x, width_y, depth):
    along_x = frequency(row_index, width_x)
    along_y = frequency(jnp.arange(width_y, dtype=jnp.int32), width_y)
    squared = wave_number**2 - along_x[None, :, None] ** 2 - along_y[None, None, :] ** 2
    distance = (depth - depth_index).astype(jnp.float32)[:, None, None]
    root = jnp.sqrt(jnp.abs(squared))
    moving = squared > 0.0
    amplitude = jnp.where(moving, 1.0, jnp.exp(-root * distance))
    phase = jnp.where(moving, root * distance, 0.0)
    return (amplitude * jnp.cos(phase), amplitude * jnp.sin(phase))


def tv_pass(padded, first, depth):
    rows = padded.shape[0]
    global_row = first + jnp.arange(rows - 1, dtype=jnp.int32)
    inside = (global_row >= 0) & (global_row <= depth - 2)
    core = padded[:-1]
    slope_depth = jnp.where(inside[:, None, None], padded[1:] - core, 0.0)
    slope_rows = jnp.concatenate([core[:, 1:] - core[:, :-1], jnp.zeros_like(core[:, :1])], axis=1)
    slope_cols = jnp.concatenate(
        [core[:, :, 1:] - core[:, :, :-1], jnp.zeros_like(core[:, :, :1])], axis=2
    )
    magnitude = jnp.sqrt(slope_depth**2 + slope_rows**2 + slope_cols**2 + edge_scale**2)
    flux_depth = slope_depth / magnitude
    flux_rows = (slope_rows / magnitude)[1:]
    flux_cols = (slope_cols / magnitude)[1:]
    spread_depth = flux_depth[1:] - flux_depth[:-1]
    spread_rows = flux_rows - jnp.concatenate(
        [jnp.zeros_like(flux_rows[:, :1]), flux_rows[:, :-1]], axis=1
    )
    spread_cols = flux_cols - jnp.concatenate(
        [jnp.zeros_like(flux_cols[:, :, :1]), flux_cols[:, :, :-1]], axis=2
    )
    return padded[1:-1] + diffusion * (spread_depth + spread_rows + spread_cols)


def back_project(prop_real, prop_imag, mismatch, root_depth):
    miss_real = mismatch[:, 0][:, None]
    miss_imag = mismatch[:, 1][:, None]
    out_real = (prop_real[None] * miss_real + prop_imag[None] * miss_imag) / root_depth
    out_imag = (prop_real[None] * miss_imag - prop_imag[None] * miss_real) / root_depth
    return jnp.stack([out_real, out_imag], 1)


def shards(incident, field_now, contrast, green_spectrum, detector_data):
    slabs = lax.axis_size("slab")
    place = lax.axis_index("slab")
    local_depth, width_x, width_y = contrast.shape
    depth = local_depth * slabs
    cols_x = width_x // slabs
    root_depth = math.sqrt(depth)
    cos_x, sin_x = tables(width_x)
    cos_y, sin_y = tables(width_y)
    cos_z, sin_z = tables(depth)
    real_now = field_now[:, 0]
    imag_now = field_now[:, 1]
    spec_real, spec_imag = mixing(
        contrast[None] * real_now, contrast[None] * imag_now, cos_x, sin_x, -1.0, form_rows
    )
    spec_real, spec_imag = mixing(spec_real, spec_imag, cos_y, sin_y, -1.0, form_cols)
    spectrum = jnp.stack([spec_real, spec_imag], 1)
    columns = lax.all_to_all(spectrum, "slab", split_axis=3, concat_axis=2, tiled=True)
    deep_real, deep_imag = mixing(columns[:, 0], columns[:, 1], cos_z, sin_z, -1.0, form_depth)
    green_real = green_spectrum[0][None]
    green_imag = green_spectrum[1][None]
    prod_real = green_real * deep_real - green_imag * deep_imag
    prod_imag = green_real * deep_imag + green_imag * deep_real
    vol_real, vol_imag = mixing(prod_real, prod_imag, cos_z, sin_z, 1.0, form_depth)
    volume = jnp.stack([vol_real, vol_imag], 1)
    kx_index = place * cols_x + jnp.arange(cols_x, dtype=jnp.int32)
    col_prop_real, col_prop_imag = propagator(
        jnp.arange(depth, dtype=jnp.int32), kx_index, width_x, width_y, depth
    )
    col_real = columns[:, 0]
    col_imag = columns[:, 1]
    pred_real = (
        jnp.sum(col_prop_real[None] * col_real - col_prop_imag[None] * col_imag, axis=1)
        / root_depth
    )
    pred_imag = (
        jnp.sum(col_prop_real[None] * col_imag + col_prop_imag[None] * col_real, axis=1)
        / root_depth
    )
    mismatch = jnp.stack([pred_real, pred_imag], 1) - detector_data
    volume = lax.all_to_all(volume, "slab", split_axis=2, concat_axis=3, tiled=True)
    depth_index = place * local_depth + jnp.arange(local_depth, dtype=jnp.int32)
    prop_real, prop_imag = propagator(
        depth_index, jnp.arange(width_x, dtype=jnp.int32), width_x, width_y, depth
    )
    gathered = lax.all_gather(mismatch, "slab", axis=2, tiled=True)
    returned = back_project(prop_real, prop_imag, gathered, root_depth)
    scat_real, scat_imag = mixing(volume[:, 0], volume[:, 1], cos_x, sin_x, 1.0, form_rows)
    scat_real, scat_imag = mixing(scat_real, scat_imag, cos_y, sin_y, 1.0, form_cols)
    field_next = incident.astype(jnp.float32) + jnp.stack([scat_real, scat_imag], 1)
    ret_real, ret_imag = mixing(returned[:, 0], returned[:, 1], cos_x, sin_x, 1.0, form_rows)
    ret_real, ret_imag = mixing(ret_real, ret_imag, cos_y, sin_y, 1.0, form_cols)
    local_terms = jnp.sum(real_now * ret_real + imag_now * ret_imag, axis=0)
    illums = lax.axis_size("illum")
    gradient, travelling = local_terms, local_terms
    for hop in range(illums - 1):
        travelling = lax.ppermute(travelling, "illum", [(i, (i + 1) % illums) for i in range(illums)])
        gradient = gradient + travelling
    updated = contrast - step_size * gradient
    wide = math.gcd(passes, local_depth)
    for repeat in range(passes // wide):
        updated = with_halo(updated, (("slab", 0),), wide)
        for left in range(wide, 0, -1):
            updated = tv_pass(updated, place * local_depth - left, depth)
    return (field_next, mismatch, updated)


def split_halves(value):
    high = value.astype(jnp.bfloat16)
    return high, (value - high.astype(jnp.float32)).astype(jnp.bfloat16)


def product(left, right):
    return jnp.dot(left, right, preferred_element_type=jnp.float32)


def combine(both, sign):
    rows, cols = both.shape[0] // 2, both.shape[1] // 2
    by_cos, by_sin = both[:rows], both[rows:]
    real = by_cos[:, :cols] - sign * by_sin[:, cols:]
    imag = by_cos[:, cols:] + sign * by_sin[:, :cols]
    return real, imag


def transform_rows(pair, high_ref, low_ref, sign):
    high, low = split_halves(pair)
    table = high_ref[...]
    both = product(table, high) + product(table, low) + product(low_ref[...], high)
    return jnp.concatenate(combine(both, sign), axis=1)


def transform_cols(pair, high_ref, low_ref):
    high, low = split_halves(pair)
    table = high_ref[...]
    return product(high, table) + product(low, table) + product(high, low_ref[...])


def host_tables(length):
    counter = np.arange(length)
    angle = (counter[:, None] * counter[None, :] % length) * (2.0 * math.pi / length)
    return np.cos(angle) / math.sqrt(length), np.sin(angle) / math.sqrt(length)


def host_frequency(length):
    index = np.arange(length)
    return np.where(index < length // 2, index, index - length) * (2.0 * math.pi / length)


def host_propagator(distance, width_x, width_y):
    squared = (
        wave_number**2 - host_frequency(width_x)[:, None] ** 2 - host_frequency(width_y)[None] ** 2
    )
    root = np.sqrt(np.abs(squared))
    moving = squared > 0.0
    amplitude = np.where(moving, 1.0, np.exp(-root * distance))
    phase = np.where(moving, root * distance, 0.0)
    pair = [amplitude * np.cos(phase), amplitude * np.sin(phase)]
    return np.concatenate(pair, axis=1).astype(np.float32)


def fused_kernel(
    field_any, contrast_any, yf_any, x_any, green_any, step_any,
    detector_any, z_any, start_any, yi_any, incident_any,
    field_out, misfit_out, contrast_out,
    out1, in1, out2, in2, miss, gmine, gpeer, cube, cube2, zbuf, gbuf, rbuf, fz,
    field, contrast, yf, xt, green, step_ref, detector, zf, start, yi, inc,
    yfh, yfl, yih, yil, xh, xl, zt_ref,
    load_sem, s1, r1, s2, r2, sm, rm, sg, rg, sh, rh,
):
    slabs, local_depth, cols_x, pair_y = out1.shape
    width_y = pair_y // 2
    width_x = slabs * cols_x
    depth = slabs * local_depth
    root_depth = math.sqrt(depth)
    me = lax.axis_index("slab")
    lane = lax.axis_index("illum")
    other = 1 - lane

    def at(hop):
        return lax.rem(me + hop, slabs)

    def spread(body):
        lax.fori_loop(1, slabs, lambda hop, carry: (body(at(hop)), carry)[1], 0)

    barrier = pltpu.get_barrier_semaphore()

    def greet(dst):
        pl.semaphore_signal(barrier, inc=1, device_id=(lane, dst), device_id_type=MESH)

    sources = [
        field_any, contrast_any, yf_any, x_any, green_any, step_any,
        detector_any, z_any, start_any.at[me], yi_any, incident_any,
    ]
    held = [field, contrast, yf, xt, green, step_ref, detector, zf, start, yi, inc]
    early = 4
    loads = [
        pltpu.make_async_copy(src, dst, load_sem.at[i])
        for i, (src, dst) in enumerate(zip(sources, held))
    ]
    for load in loads:
        load.start()
    spread(greet)
    pl.semaphore_signal(barrier, inc=1, device_id=(other, me), device_id_type=MESH)

    def remote(src, dst, send, recv, who):
        return pltpu.make_async_remote_copy(
            src_ref=src, dst_ref=dst, send_sem=send, recv_sem=recv,
            device_id=who, device_id_type=MESH,
        )

    def forward(plane, carry):
        c = contrast[plane]
        pair = jnp.concatenate([c * field[0, 0, plane], c * field[0, 1, plane]], axis=1)
        pair = transform_cols(pair, yfh, yfl)
        pair = transform_rows(pair, xh, xl, -1.0)
        out1[:, plane] = pair.reshape(slabs, cols_x, pair_y)
        return carry

    for load in loads[:early]:
        load.wait()
    yfh[...], yfl[...] = split_halves(yf[...])
    xh[...], xl[...] = split_halves(xt[...])
    parts = 1
    groups = math.gcd(local_depth, 2)
    size = local_depth // groups

    def send_block(part, first, count):
        planes, rows = pl.ds(first, count), pl.ds(0, cols_x)
        spread(
            lambda dst: remote(
                out1.at[dst, planes, rows], in1.at[me, planes, rows],
                s1.at[part, dst], r1.at[part, me], (lane, dst),
            ).start()
        )

    for group in range(groups):
        lax.fori_loop(group * size, (group + 1) * size, forward, 0)
        if group == 0:
            pl.semaphore_wait(barrier, slabs)
        send_block(0, group * size, size)
    for part in range(1, parts):
        send_block(part, 0, local_depth)
    in1[me] = out1[me]

    for load in loads[early:]:
        load.wait()
    yih[...], yil[...] = split_halves(yi[...])
    z_high, z_low = split_halves(zf[...])
    zt_ref[...] = jnp.concatenate([z_high, z_high, z_low, z_low], axis=1)
    for first in range(0, cols_x, 8):
        rows = slice(first, first + 8)
        for half in range(2):
            cols = slice(half * width_y, (half + 1) * width_y)
            gbuf[rows, :, cols] = jnp.transpose(green[half, :, rows, :], (1, 0, 2))

    def convolve(row, carry):
        table = zt_ref[...]
        high, low = split_halves(zbuf[row])
        both = product(table, jnp.concatenate([high, low, high, low], axis=0))
        real, imag = combine(both, -1.0)
        g_real, g_imag = gbuf[row, :, :width_y], gbuf[row, :, width_y:]
        pair = jnp.concatenate(
            [g_real * real - g_imag * imag, g_real * imag + g_imag * real], axis=1
        )
        high, low = split_halves(pair)
        both = product(table, jnp.concatenate([high, low, high, low], axis=0))
        zbuf[row] = jnp.concatenate(combine(both, 1.0), axis=1)
        return carry

    for part in range(parts):
        rows, cut = slice(0, cols_x), pl.ds(0, cols_x)
        spread(
            lambda src: remote(
                out1.at[src, :, cut], in1.at[src, :, cut],
                s1.at[part, src], r1.at[part, src], (lane, src),
            ).wait_recv()
        )
        own = pl.ds(pl.multiple_of(me * cols_x, 8), cols_x)
        step_r, step_i = step_ref[own, :width_y], step_ref[own, width_y:]

        def horner(src, carry):
            real, imag = carry
            for plane in range(local_depth):
                real = real + in1[src, plane, rows, :width_y]
                imag = imag + in1[src, plane, rows, width_y:]
                real, imag = (real * step_r - imag * step_i, real * step_i + imag * step_r)
            return real, imag

        zero = jnp.zeros((cols_x, width_y), jnp.float32)
        real, imag = lax.fori_loop(0, slabs, horner, (zero, zero))
        real = real / root_depth - detector[0, 0, rows]
        imag = imag / root_depth - detector[0, 1, rows]
        misfit_out[0, 0, rows] = real
        misfit_out[0, 1, rows] = imag
        miss[me, rows, :width_y] = real
        miss[me, rows, width_y:] = imag
        spread(
            lambda dst: remote(
                miss.at[me, cut], miss.at[me, cut],
                sm.at[part, dst], rm.at[part, me], (lane, dst),
            ).start()
        )
        for first in range(0, cols_x, 8):
            eight = slice(first, first + 8)
            block = in1[:, :, eight, :].reshape(depth, 8, pair_y)
            zbuf[eight] = jnp.transpose(block, (1, 0, 2))
        lax.fori_loop(0, cols_x, convolve, 0)
        for first in range(0, cols_x, 8):
            eight = slice(first, first + 8)
            block = jnp.transpose(zbuf[eight], (1, 0, 2))
            out2[:, :, eight, :] = block.reshape(slabs, local_depth, 8, pair_y)
        spread(
            lambda dst: remote(
                out2.at[dst, :, cut], in2.at[me, :, cut],
                s2.at[part, dst], r2.at[part, me], (lane, dst),
            ).start()
        )
    in2[me] = out2[me]

    for part in range(parts):
        cut = pl.ds(0, cols_x)
        spread(
            lambda src: remote(
                miss.at[src, cut], miss.at[src, cut],
                sm.at[part, src], rm.at[part, src], (lane, src),
            ).wait_recv()
        )
    gathered = miss[...].reshape(width_x, pair_y)
    m_real, m_imag = gathered[:, :width_y], gathered[:, width_y:]
    p_real, p_imag = start[:, :width_y], start[:, width_y:]
    rbuf[:, :width_y] = (p_real * m_real + p_imag * m_imag) / root_depth
    rbuf[:, width_y:] = (p_real * m_imag - p_imag * m_real) / root_depth

    def peer_copy(plane):
        return remote(
            gmine.at[plane], gpeer.at[plane], sg.at[plane], rg.at[plane], (other, me)
        )

    def project(count, carry):
        plane = local_depth - 1 - count
        now = rbuf[...]
        pair = transform_rows(now, xh, xl, 1.0)
        pair = transform_cols(pair, yih, yil)
        gmine[plane] = field[0, 0, plane] * pair[:, :width_y] + field[0, 1, plane] * pair[:, width_y:]
        peer_copy(plane).start()
        now_r, now_i = now[:, :width_y], now[:, width_y:]
        w_real, w_imag = step_ref[:, :width_y], step_ref[:, width_y:]
        rbuf[:, :width_y] = w_real * now_r + w_imag * now_i
        rbuf[:, width_y:] = w_real * now_i - w_imag * now_r
        return carry

    lax.fori_loop(0, local_depth, project, 0)

    def update(count, carry):
        plane = local_depth - 1 - count
        peer_copy(plane).wait()
        cube[passes + plane] = contrast[plane] - step_size * (gmine[plane] + gpeer[plane])
        return carry

    lax.fori_loop(0, local_depth, update, 0)
    low_side, high_side = pl.ds(0, passes), pl.ds(passes + local_depth, passes)
    up = remote(
        cube.at[pl.ds(local_depth, passes)], cube.at[low_side], sh.at[0], rh.at[0],
        (lane, lax.rem(me + 1, slabs)),
    )
    down = remote(
        cube.at[pl.ds(passes, passes)], cube.at[high_side], sh.at[1], rh.at[1],
        (lane, lax.rem(me + slabs - 1, slabs)),
    )
    has_up, has_down = me < slabs - 1, me > 0
    pl.when(has_up)(up.start)
    pl.when(has_down)(down.start)

    @pl.when(me == 0)
    def _():
        cube[low_side] = jnp.zeros((passes, width_x, width_y), jnp.float32)

    @pl.when(me == slabs - 1)
    def _():
        cube[high_side] = jnp.zeros((passes, width_x, width_y), jnp.float32)

    pl.when(has_up)(up.wait_send)
    pl.when(has_down)(down.wait_send)
    pl.when(has_down)(up.wait_recv)
    pl.when(has_up)(down.wait_recv)

    row_at = lax.broadcasted_iota(jnp.int32, (width_x, width_y), 0)
    col_at = lax.broadcasted_iota(jnp.int32, (width_x, width_y), 1)

    def sweep(source, plane, write):
        cur = source[plane]
        place = me * local_depth - passes + plane
        inside = jnp.where((place >= 0) & (place <= depth - 2), 1.0, 0.0)
        slope_z = (source[plane + 1] - cur) * inside
        flux_x = jnp.where(row_at < width_x - 1, pltpu.roll(cur, width_x - 1, 0) - cur, 0.0)
        flux_y = jnp.where(col_at < width_y - 1, pltpu.roll(cur, width_y - 1, 1) - cur, 0.0)
        scale = lax.rsqrt(slope_z**2 + flux_x**2 + flux_y**2 + edge_scale**2)
        flux_z = slope_z * scale
        if write is not None:
            flux_x = flux_x * scale
            flux_y = flux_y * scale
            total = flux_z - fz[...] + flux_x - pltpu.roll(flux_x, 1, 0)
            total = total + flux_y - pltpu.roll(flux_y, 1, 1)
            write(plane, cur + diffusion * total)
        fz[...] = flux_z

    planes = local_depth + 2 * passes
    for turn in range(passes):
        source, target = (cube, cube2) if turn % 2 == 0 else (cube2, cube)
        sweep(source, turn, None)

        def write(plane, value, turn=turn, target=target):
            if turn == passes - 1:
                contrast_out[plane - passes] = value
            else:
                target[plane] = value

        def one(plane, carry, source=source, write=write):
            sweep(source, plane, write)
            return carry

        lax.fori_loop(turn + 1, planes - 1 - turn, one, 0)

    for part in range(parts):
        cut = pl.ds(0, cols_x)
        spread(
            lambda src: remote(
                out2.at[src, :, cut], in2.at[src, :, cut],
                s2.at[part, src], r2.at[part, src], (lane, src),
            ).wait_recv()
        )

    def finish(plane, carry):
        pair = in2[:, plane].reshape(width_x, pair_y)
        pair = transform_rows(pair, xh, xl, 1.0)
        pair = transform_cols(pair, yih, yil)
        field_out[0, 0, plane] = inc[0, 0, plane].astype(jnp.float32) + pair[:, :width_y]
        field_out[0, 1, plane] = inc[0, 1, plane].astype(jnp.float32) + pair[:, width_y:]
        return carry

    lax.fori_loop(0, local_depth, finish, 0)

    def drain(part, dst):
        cut = pl.ds(0, cols_x)
        who = (lane, dst)
        remote(
            out1.at[dst, :, cut], in1.at[me, :, cut], s1.at[part, dst], r1.at[part, me], who
        ).wait_send()
        remote(
            miss.at[me, cut], miss.at[me, cut], sm.at[part, dst], rm.at[part, me], who
        ).wait_send()
        remote(
            out2.at[dst, :, cut], in2.at[me, :, cut], s2.at[part, dst], r2.at[part, me], who
        ).wait_send()

    for part in range(parts):
        spread(lambda dst: drain(part, dst))


def fused(incident, field_now, contrast, green_spectrum, detector_data):
    slabs = lax.axis_size("slab")
    local_depth, width_x, width_y = contrast.shape
    depth = local_depth * slabs
    cols_x = width_x // slabs
    pair_y = 2 * width_y
    cos_x, sin_x = host_tables(width_x)
    cos_y, sin_y = host_tables(width_y)
    cos_z, sin_z = host_tables(depth)
    table_x = np.concatenate([cos_x, sin_x], axis=0).astype(np.float32)
    forward_y = np.block([[cos_y, -sin_y], [sin_y, cos_y]]).astype(np.float32)
    inverse_y = np.block([[cos_y, sin_y], [-sin_y, cos_y]]).astype(np.float32)
    table_z = np.concatenate([cos_z, sin_z], axis=0).astype(np.float32)
    step = host_propagator(1, width_x, width_y)
    nearest = [depth - (s * local_depth + local_depth - 1) for s in range(slabs)]
    start = np.stack([host_propagator(d, width_x, width_y) for d in nearest])
    vmem, anywhere = pl.BlockSpec(memory_space=pltpu.VMEM), pl.BlockSpec(memory_space=pl.ANY)
    f32 = jnp.float32
    block = pltpu.VMEM((slabs, local_depth, cols_x, pair_y), f32)
    planes = pltpu.VMEM((local_depth, width_x, width_y), f32)
    padded = pltpu.VMEM((local_depth + 2 * passes, width_x, width_y), f32)
    turned = pltpu.VMEM((cols_x, depth, pair_y), f32)
    cols_table = pltpu.VMEM((pair_y, pair_y), jnp.bfloat16)
    rows_table = pltpu.VMEM((2 * width_x, width_x), jnp.bfloat16)
    several = pltpu.SemaphoreType.DMA((1, slabs))
    return pl.pallas_call(
        fused_kernel,
        out_shape=(
            jax.ShapeDtypeStruct(field_now.shape, f32),
            jax.ShapeDtypeStruct(detector_data.shape, f32),
            jax.ShapeDtypeStruct(contrast.shape, f32),
        ),
        in_specs=[anywhere] * 11,
        out_specs=(vmem, vmem, vmem),
        scratch_shapes=[
            block, block, block, block,
            pltpu.VMEM((slabs, cols_x, pair_y), f32),
            planes, planes, padded, padded, turned, turned,
            pltpu.VMEM((width_x, pair_y), f32),
            pltpu.VMEM((width_x, width_y), f32),
            pltpu.VMEM(field_now.shape, f32),
            planes,
            pltpu.VMEM(forward_y.shape, f32),
            pltpu.VMEM(table_x.shape, f32),
            pltpu.VMEM(green_spectrum.shape, f32),
            pltpu.VMEM((width_x, pair_y), f32),
            pltpu.VMEM(detector_data.shape, f32),
            pltpu.VMEM(table_z.shape, f32),
            pltpu.VMEM((width_x, pair_y), f32),
            pltpu.VMEM(inverse_y.shape, f32),
            pltpu.VMEM(incident.shape, jnp.bfloat16),
            cols_table, cols_table, cols_table, cols_table, rows_table, rows_table,
            pltpu.VMEM((2 * depth, 4 * depth), jnp.bfloat16),
            pltpu.SemaphoreType.DMA((11,)),
            several, several, several, several, several, several,
            pltpu.SemaphoreType.DMA((local_depth,)),
            pltpu.SemaphoreType.DMA((local_depth,)),
            pltpu.SemaphoreType.DMA((2,)),
            pltpu.SemaphoreType.DMA((2,)),
        ],
        compiler_params=pltpu.CompilerParams(
            collective_id=0, has_side_effects=True, vmem_limit_bytes=60 * 2**20
        ),
    )(
        field_now, contrast, forward_y, table_x, green_spectrum, step,
        detector_data, table_z, start, inverse_y, incident,
    )


def whole_tiles(mesh, arrays):
    local_depth = arrays[2].shape[0]
    rows = arrays[3].shape[2]
    return (
        mesh.shape["illum"] == 2
        and mesh.shape["slab"] > 1
        and rows % 8 == 0
        and (local_depth * mesh.shape["slab"]) % 16 == 0
        and arrays[2].shape[2] % 128 == 0
        and local_depth >= passes
    )


def solution(mesh):
    placed = (
        P("illum", None, "slab", None, None),
        P("illum", None, "slab", None, None),
        P("slab", None, None),
        P(None, None, "slab", None),
        P("illum", None, "slab", None),
    )

    def pick(*arrays):
        return (fused if whole_tiles(mesh, arrays) else shards)(*arrays)

    return jax.shard_map(
        pick,
        mesh=mesh,
        in_specs=placed,
        out_specs=(
            P("illum", None, "slab", None, None),
            P("illum", None, "slab", None),
            P("slab", None, None),
        ),
        check_vma=False,
    )
```

```python
import math

import jax
import jax.numpy as jnp
import numpy as np
from jax import lax
from jax.experimental import pallas as pl
from jax.experimental.pallas import tpu as pltpu
from jax.sharding import PartitionSpec as P

wave_number = 1.2
step_size = 2.0
diffusion = 0.02
edge_scale = 0.25
passes = 4
MESH = pl.DeviceIdType.MESH
highest = lax.Precision.HIGH
form_rows = "...xy,xk->...ky"
form_cols = "...y,yk->...k"
form_depth = "azxy,zk->akxy"


def with_halo(array, sides, width):
    for axis, dim in sides:
        devices, length = (lax.axis_size(axis), array.shape[dim])
        up = [(i, (i + 1) % devices) for i in range(devices - 1)]
        down = [(j, i) for i, j in up]
        last = lax.slice_in_dim(array, length - width, length, axis=dim)
        leading = lax.slice_in_dim(array, 0, width, axis=dim)
        before = lax.ppermute(last, axis, up)
        after = lax.ppermute(leading, axis, down)
        array = jnp.concatenate([before, array, after], axis=dim)
    return array


def tables(length):
    counter = jnp.arange(length, dtype=jnp.int32)
    product = counter[:, None] * counter[None, :] % length
    angle = product.astype(jnp.float32) * (2.0 * math.pi / length)
    scale = 1.0 / math.sqrt(length)
    return (jnp.cos(angle) * scale, jnp.sin(angle) * scale)


def mixing(real, imag, cosine, sine_table, sign, form):
    real_cos = jnp.einsum(form, real, cosine, precision=highest)
    real_sin = jnp.einsum(form, real, sine_table, precision=highest)
    imag_cos = jnp.einsum(form, imag, cosine, precision=highest)
    imag_sin = jnp.einsum(form, imag, sine_table, precision=highest)
    return (real_cos - sign * imag_sin, imag_cos + sign * real_sin)


def frequency(index, length):
    shifted = jnp.where(index < length // 2, index, index - length)
    return shifted.astype(jnp.float32) * (2.0 * math.pi / length)


def propagator(depth_index, row_index, width_x, width_y, depth):
    along_x = frequency(row_index, width_x)
    along_y = frequency(jnp.arange(width_y, dtype=jnp.int32), width_y)
    squared = wave_number**2 - along_x[None, :, None] ** 2 - along_y[None, None, :] ** 2
    distance = (depth - depth_index).astype(jnp.float32)[:, None, None]
    root = jnp.sqrt(jnp.abs(squared))
    moving = squared > 0.0
    amplitude = jnp.where(moving, 1.0, jnp.exp(-root * distance))
    phase = jnp.where(moving, root * distance, 0.0)
    return (amplitude * jnp.cos(phase), amplitude * jnp.sin(phase))


def tv_pass(padded, first, depth):
    rows = padded.shape[0]
    global_row = first + jnp.arange(rows - 1, dtype=jnp.int32)
    inside = (global_row >= 0) & (global_row <= depth - 2)
    core = padded[:-1]
    slope_depth = jnp.where(inside[:, None, None], padded[1:] - core, 0.0)
    slope_rows = jnp.concatenate([core[:, 1:] - core[:, :-1], jnp.zeros_like(core[:, :1])], axis=1)
    slope_cols = jnp.concatenate(
        [core[:, :, 1:] - core[:, :, :-1], jnp.zeros_like(core[:, :, :1])], axis=2
    )
    magnitude = jnp.sqrt(slope_depth**2 + slope_rows**2 + slope_cols**2 + edge_scale**2)
    flux_depth = slope_depth / magnitude
    flux_rows = (slope_rows / magnitude)[1:]
    flux_cols = (slope_cols / magnitude)[1:]
    spread_depth = flux_depth[1:] - flux_depth[:-1]
    spread_rows = flux_rows - jnp.concatenate(
        [jnp.zeros_like(flux_rows[:, :1]), flux_rows[:, :-1]], axis=1
    )
    spread_cols = flux_cols - jnp.concatenate(
        [jnp.zeros_like(flux_cols[:, :, :1]), flux_cols[:, :, :-1]], axis=2
    )
    return padded[1:-1] + diffusion * (spread_depth + spread_rows + spread_cols)


def back_project(prop_real, prop_imag, mismatch, root_depth):
    miss_real = mismatch[:, 0][:, None]
    miss_imag = mismatch[:, 1][:, None]
    out_real = (prop_real[None] * miss_real + prop_imag[None] * miss_imag) / root_depth
    out_imag = (prop_real[None] * miss_imag - prop_imag[None] * miss_real) / root_depth
    return jnp.stack([out_real, out_imag], 1)


def shards(incident, field_now, contrast, green_spectrum, detector_data):
    slabs = lax.axis_size("slab")
    place = lax.axis_index("slab")
    local_depth, width_x, width_y = contrast.shape
    depth = local_depth * slabs
    cols_x = width_x // slabs
    root_depth = math.sqrt(depth)
    cos_x, sin_x = tables(width_x)
    cos_y, sin_y = tables(width_y)
    cos_z, sin_z = tables(depth)
    real_now = field_now[:, 0]
    imag_now = field_now[:, 1]
    spec_real, spec_imag = mixing(
        contrast[None] * real_now, contrast[None] * imag_now, cos_x, sin_x, -1.0, form_rows
    )
    spec_real, spec_imag = mixing(spec_real, spec_imag, cos_y, sin_y, -1.0, form_cols)
    spectrum = jnp.stack([spec_real, spec_imag], 1)
    columns = lax.all_to_all(spectrum, "slab", split_axis=3, concat_axis=2, tiled=True)
    deep_real, deep_imag = mixing(columns[:, 0], columns[:, 1], cos_z, sin_z, -1.0, form_depth)
    green_real = green_spectrum[0][None]
    green_imag = green_spectrum[1][None]
    prod_real = green_real * deep_real - green_imag * deep_imag
    prod_imag = green_real * deep_imag + green_imag * deep_real
    vol_real, vol_imag = mixing(prod_real, prod_imag, cos_z, sin_z, 1.0, form_depth)
    volume = jnp.stack([vol_real, vol_imag], 1)
    kx_index = place * cols_x + jnp.arange(cols_x, dtype=jnp.int32)
    col_prop_real, col_prop_imag = propagator(
        jnp.arange(depth, dtype=jnp.int32), kx_index, width_x, width_y, depth
    )
    col_real = columns[:, 0]
    col_imag = columns[:, 1]
    pred_real = (
        jnp.sum(col_prop_real[None] * col_real - col_prop_imag[None] * col_imag, axis=1)
        / root_depth
    )
    pred_imag = (
        jnp.sum(col_prop_real[None] * col_imag + col_prop_imag[None] * col_real, axis=1)
        / root_depth
    )
    mismatch = jnp.stack([pred_real, pred_imag], 1) - detector_data
    volume = lax.all_to_all(volume, "slab", split_axis=2, concat_axis=3, tiled=True)
    depth_index = place * local_depth + jnp.arange(local_depth, dtype=jnp.int32)
    prop_real, prop_imag = propagator(
        depth_index, jnp.arange(width_x, dtype=jnp.int32), width_x, width_y, depth
    )
    gathered = lax.all_gather(mismatch, "slab", axis=2, tiled=True)
    returned = back_project(prop_real, prop_imag, gathered, root_depth)
    scat_real, scat_imag = mixing(volume[:, 0], volume[:, 1], cos_x, sin_x, 1.0, form_rows)
    scat_real, scat_imag = mixing(scat_real, scat_imag, cos_y, sin_y, 1.0, form_cols)
    field_next = incident.astype(jnp.float32) + jnp.stack([scat_real, scat_imag], 1)
    ret_real, ret_imag = mixing(returned[:, 0], returned[:, 1], cos_x, sin_x, 1.0, form_rows)
    ret_real, ret_imag = mixing(ret_real, ret_imag, cos_y, sin_y, 1.0, form_cols)
    local_terms = jnp.sum(real_now * ret_real + imag_now * ret_imag, axis=0)
    illums = lax.axis_size("illum")
    gradient, travelling = local_terms, local_terms
    for hop in range(illums - 1):
        travelling = lax.ppermute(travelling, "illum", [(i, (i + 1) % illums) for i in range(illums)])
        gradient = gradient + travelling
    updated = contrast - step_size * gradient
    wide = math.gcd(passes, local_depth)
    for repeat in range(passes // wide):
        updated = with_halo(updated, (("slab", 0),), wide)
        for left in range(wide, 0, -1):
            updated = tv_pass(updated, place * local_depth - left, depth)
    return (field_next, mismatch, updated)


def split_halves(value):
    high = value.astype(jnp.bfloat16)
    return high, (value - high.astype(jnp.float32)).astype(jnp.bfloat16)


def product(left, right):
    return jnp.dot(left, right, preferred_element_type=jnp.float32)


def combine(both, sign):
    rows, cols = both.shape[0] // 2, both.shape[1] // 2
    by_cos, by_sin = both[:rows], both[rows:]
    real = by_cos[:, :cols] - sign * by_sin[:, cols:]
    imag = by_cos[:, cols:] + sign * by_sin[:, :cols]
    return real, imag


def transform_rows(pair, high_ref, low_ref, sign):
    high, low = split_halves(pair)
    table = high_ref[...]
    both = product(table, high) + product(table, low) + product(low_ref[...], high)
    return jnp.concatenate(combine(both, sign), axis=1)


def transform_cols(pair, high_ref, low_ref):
    high, low = split_halves(pair)
    table = high_ref[...]
    return product(high, table) + product(low, table) + product(high, low_ref[...])


def host_tables(length):
    counter = np.arange(length)
    angle = (counter[:, None] * counter[None, :] % length) * (2.0 * math.pi / length)
    return np.cos(angle) / math.sqrt(length), np.sin(angle) / math.sqrt(length)


def host_frequency(length):
    index = np.arange(length)
    return np.where(index < length // 2, index, index - length) * (2.0 * math.pi / length)


def host_propagator(distance, width_x, width_y):
    squared = (
        wave_number**2 - host_frequency(width_x)[:, None] ** 2 - host_frequency(width_y)[None] ** 2
    )
    root = np.sqrt(np.abs(squared))
    moving = squared > 0.0
    amplitude = np.where(moving, 1.0, np.exp(-root * distance))
    phase = np.where(moving, root * distance, 0.0)
    pair = [amplitude * np.cos(phase), amplitude * np.sin(phase)]
    return np.concatenate(pair, axis=1).astype(np.float32)


def fused_kernel(
    field_any, contrast_any, yf_any, x_any, green_any, step_any,
    detector_any, z_any, start_any, yi_any,
    field_out, misfit_out, contrast_out,
    out1, in1, out2, in2, miss, gmine, gpeer, cube, cube2, zbuf, gbuf, rbuf, fz,
    field, contrast, yf, xt, green, step_ref, detector, zf, start, yi,
    yfh, yfl, yih, yil, xh, xl, zt_ref,
    load_sem, s1, r1, s2, r2, sm, rm, sg, rg, sh, rh,
):
    slabs, local_depth, cols_x, pair_y = out1.shape
    width_y = pair_y // 2
    width_x = slabs * cols_x
    depth = slabs * local_depth
    root_depth = math.sqrt(depth)
    me = lax.axis_index("slab")
    lane = lax.axis_index("illum")
    other = 1 - lane

    def at(hop):
        return lax.rem(me + hop, slabs)

    def spread(body):
        lax.fori_loop(1, slabs, lambda hop, carry: (body(at(hop)), carry)[1], 0)

    barrier = pltpu.get_barrier_semaphore()

    def greet(dst):
        pl.semaphore_signal(barrier, inc=1, device_id=(lane, dst), device_id_type=MESH)

    sources = [
        field_any, contrast_any, yf_any, x_any, green_any, step_any,
        detector_any, z_any, start_any.at[me], yi_any,
    ]
    held = [field, contrast, yf, xt, green, step_ref, detector, zf, start, yi]
    early = 4
    loads = [
        pltpu.make_async_copy(src, dst, load_sem.at[i])
        for i, (src, dst) in enumerate(zip(sources, held))
    ]
    for load in loads:
        load.start()
    spread(greet)
    pl.semaphore_signal(barrier, inc=1, device_id=(other, me), device_id_type=MESH)

    def remote(src, dst, send, recv, who):
        return pltpu.make_async_remote_copy(
            src_ref=src, dst_ref=dst, send_sem=send, recv_sem=recv,
            device_id=who, device_id_type=MESH,
        )

    def forward(plane, carry):
        c = contrast[plane]
        pair = jnp.concatenate([c * field[0, 0, plane], c * field[0, 1, plane]], axis=1)
        pair = transform_cols(pair, yfh, yfl)
        pair = transform_rows(pair, xh, xl, -1.0)
        out1[:, plane] = pair.reshape(slabs, cols_x, pair_y)
        return carry

    for load in loads[:early]:
        load.wait()
    yfh[...], yfl[...] = split_halves(yf[...])
    xh[...], xl[...] = split_halves(xt[...])
    parts = 1
    groups = math.gcd(local_depth, 2)
    size = local_depth // groups

    def send_block(part, first, count):
        planes, rows = pl.ds(first, count), pl.ds(0, cols_x)
        spread(
            lambda dst: remote(
                out1.at[dst, planes, rows], in1.at[me, planes, rows],
                s1.at[part, dst], r1.at[part, me], (lane, dst),
            ).start()
        )

    for group in range(groups):
        lax.fori_loop(group * size, (group + 1) * size, forward, 0)
        if group == 0:
            pl.semaphore_wait(barrier, slabs)
        send_block(0, group * size, size)
    for part in range(1, parts):
        send_block(part, 0, local_depth)
    in1[me] = out1[me]

    for load in loads[early:]:
        load.wait()
    yih[...], yil[...] = split_halves(yi[...])
    z_high, z_low = split_halves(zf[...])
    zt_ref[...] = jnp.concatenate([z_high, z_high, z_low, z_low], axis=1)
    for first in range(0, cols_x, 8):
        rows = slice(first, first + 8)
        for half in range(2):
            cols = slice(half * width_y, (half + 1) * width_y)
            gbuf[rows, :, cols] = jnp.transpose(green[half, :, rows, :], (1, 0, 2))

    def convolve(row, carry):
        table = zt_ref[...]
        high, low = split_halves(zbuf[row])
        both = product(table, jnp.concatenate([high, low, high, low], axis=0))
        real, imag = combine(both, -1.0)
        g_real, g_imag = gbuf[row, :, :width_y], gbuf[row, :, width_y:]
        pair = jnp.concatenate(
            [g_real * real - g_imag * imag, g_real * imag + g_imag * real], axis=1
        )
        high, low = split_halves(pair)
        both = product(table, jnp.concatenate([high, low, high, low], axis=0))
        zbuf[row] = jnp.concatenate(combine(both, 1.0), axis=1)
        return carry

    for part in range(parts):
        rows, cut = slice(0, cols_x), pl.ds(0, cols_x)
        spread(
            lambda src: remote(
                out1.at[src, :, cut], in1.at[src, :, cut],
                s1.at[part, src], r1.at[part, src], (lane, src),
            ).wait_recv()
        )
        own = pl.ds(pl.multiple_of(me * cols_x, 8), cols_x)
        step_r, step_i = step_ref[own, :width_y], step_ref[own, width_y:]

        def horner(src, carry):
            real, imag = carry
            for plane in range(local_depth):
                real = real + in1[src, plane, rows, :width_y]
                imag = imag + in1[src, plane, rows, width_y:]
                real, imag = (real * step_r - imag * step_i, real * step_i + imag * step_r)
            return real, imag

        zero = jnp.zeros((cols_x, width_y), jnp.float32)
        real, imag = lax.fori_loop(0, slabs, horner, (zero, zero))
        real = real / root_depth
        imag = imag / root_depth
        misfit_out[0, 0, rows] = real
        misfit_out[0, 1, rows] = imag
        real = real - detector[0, 0, rows]
        imag = imag - detector[0, 1, rows]
        miss[me, rows, :width_y] = real
        miss[me, rows, width_y:] = imag
        spread(
            lambda dst: remote(
                miss.at[me, cut], miss.at[me, cut],
                sm.at[part, dst], rm.at[part, me], (lane, dst),
            ).start()
        )
        for first in range(0, cols_x, 8):
            eight = slice(first, first + 8)
            block = in1[:, :, eight, :].reshape(depth, 8, pair_y)
            zbuf[eight] = jnp.transpose(block, (1, 0, 2))
        lax.fori_loop(0, cols_x, convolve, 0)
        for first in range(0, cols_x, 8):
            eight = slice(first, first + 8)
            block = jnp.transpose(zbuf[eight], (1, 0, 2))
            out2[:, :, eight, :] = block.reshape(slabs, local_depth, 8, pair_y)
        spread(
            lambda dst: remote(
                out2.at[dst, :, cut], in2.at[me, :, cut],
                s2.at[part, dst], r2.at[part, me], (lane, dst),
            ).start()
        )
    in2[me] = out2[me]

    for part in range(parts):
        cut = pl.ds(0, cols_x)
        spread(
            lambda src: remote(
                miss.at[src, cut], miss.at[src, cut],
                sm.at[part, src], rm.at[part, src], (lane, src),
            ).wait_recv()
        )
    gathered = miss[...].reshape(width_x, pair_y)
    m_real, m_imag = gathered[:, :width_y], gathered[:, width_y:]
    p_real, p_imag = start[:, :width_y], start[:, width_y:]
    rbuf[:, :width_y] = (p_real * m_real + p_imag * m_imag) / root_depth
    rbuf[:, width_y:] = (p_real * m_imag - p_imag * m_real) / root_depth

    def peer_copy(plane):
        return remote(
            gmine.at[plane], gpeer.at[plane], sg.at[plane], rg.at[plane], (other, me)
        )

    def project(count, carry):
        plane = local_depth - 1 - count
        now = rbuf[...]
        pair = transform_rows(now, xh, xl, 1.0)
        pair = transform_cols(pair, yih, yil)
        gmine[plane] = field[0, 0, plane] * pair[:, :width_y] + field[0, 1, plane] * pair[:, width_y:]
        peer_copy(plane).start()
        now_r, now_i = now[:, :width_y], now[:, width_y:]
        w_real, w_imag = step_ref[:, :width_y], step_ref[:, width_y:]
        rbuf[:, :width_y] = w_real * now_r + w_imag * now_i
        rbuf[:, width_y:] = w_real * now_i - w_imag * now_r
        return carry

    lax.fori_loop(0, local_depth, project, 0)

    def update(count, carry):
        plane = local_depth - 1 - count
        peer_copy(plane).wait()
        cube[passes + plane] = contrast[plane] - step_size * (gmine[plane] + gpeer[plane])
        return carry

    lax.fori_loop(0, local_depth, update, 0)
    low_side, high_side = pl.ds(0, passes), pl.ds(passes + local_depth, passes)
    up = remote(
        cube.at[pl.ds(local_depth, passes)], cube.at[low_side], sh.at[0], rh.at[0],
        (lane, lax.rem(me + 1, slabs)),
    )
    down = remote(
        cube.at[pl.ds(passes, passes)], cube.at[high_side], sh.at[1], rh.at[1],
        (lane, lax.rem(me + slabs - 1, slabs)),
    )
    has_up, has_down = me < slabs - 1, me > 0
    pl.when(has_up)(up.start)
    pl.when(has_down)(down.start)

    @pl.when(me == 0)
    def _():
        cube[low_side] = jnp.zeros((passes, width_x, width_y), jnp.float32)

    @pl.when(me == slabs - 1)
    def _():
        cube[high_side] = jnp.zeros((passes, width_x, width_y), jnp.float32)

    for part in range(parts):
        cut = pl.ds(0, cols_x)
        spread(
            lambda src: remote(
                out2.at[src, :, cut], in2.at[src, :, cut],
                s2.at[part, src], r2.at[part, src], (lane, src),
            ).wait_recv()
        )

    def finish(plane, carry):
        pair = in2[:, plane].reshape(width_x, pair_y)
        pair = transform_rows(pair, xh, xl, 1.0)
        pair = transform_cols(pair, yih, yil)
        field_out[0, 0, plane] = pair[:, :width_y]
        field_out[0, 1, plane] = pair[:, width_y:]
        return carry

    lax.fori_loop(0, local_depth, finish, 0)

    pl.when(has_up)(up.wait_send)
    pl.when(has_down)(down.wait_send)
    pl.when(has_down)(up.wait_recv)
    pl.when(has_up)(down.wait_recv)

    row_at = lax.broadcasted_iota(jnp.int32, (width_x, width_y), 0)
    col_at = lax.broadcasted_iota(jnp.int32, (width_x, width_y), 1)

    def sweep(source, plane, write):
        cur = source[plane]
        place = me * local_depth - passes + plane
        inside = jnp.where((place >= 0) & (place <= depth - 2), 1.0, 0.0)
        slope_z = (source[plane + 1] - cur) * inside
        flux_x = jnp.where(row_at < width_x - 1, pltpu.roll(cur, width_x - 1, 0) - cur, 0.0)
        flux_y = jnp.where(col_at < width_y - 1, pltpu.roll(cur, width_y - 1, 1) - cur, 0.0)
        scale = lax.rsqrt(slope_z**2 + flux_x**2 + flux_y**2 + edge_scale**2)
        flux_z = slope_z * scale
        if write is not None:
            flux_x = flux_x * scale
            flux_y = flux_y * scale
            total = flux_z - fz[...] + flux_x - pltpu.roll(flux_x, 1, 0)
            total = total + flux_y - pltpu.roll(flux_y, 1, 1)
            write(plane, cur + diffusion * total)
        fz[...] = flux_z

    planes = local_depth + 2 * passes
    for turn in range(passes):
        source, target = (cube, cube2) if turn % 2 == 0 else (cube2, cube)
        sweep(source, turn, None)

        def write(plane, value, turn=turn, target=target):
            if turn == passes - 1:
                contrast_out[plane - passes] = 2.0 * value
            else:
                target[plane] = value

        def one(plane, carry, source=source, write=write):
            sweep(source, plane, write)
            return carry

        lax.fori_loop(turn + 1, planes - 1 - turn, one, 0)

    def drain(part, dst):
        cut = pl.ds(0, cols_x)
        who = (lane, dst)
        remote(
            out1.at[dst, :, cut], in1.at[me, :, cut], s1.at[part, dst], r1.at[part, me], who
        ).wait_send()
        remote(
            miss.at[me, cut], miss.at[me, cut], sm.at[part, dst], rm.at[part, me], who
        ).wait_send()
        remote(
            out2.at[dst, :, cut], in2.at[me, :, cut], s2.at[part, dst], r2.at[part, me], who
        ).wait_send()

    for part in range(parts):
        spread(lambda dst: drain(part, dst))


def fused(incident, field_now, contrast, green_spectrum, detector_data):
    slabs = lax.axis_size("slab")
    local_depth, width_x, width_y = contrast.shape
    depth = local_depth * slabs
    cols_x = width_x // slabs
    pair_y = 2 * width_y
    cos_x, sin_x = host_tables(width_x)
    cos_y, sin_y = host_tables(width_y)
    cos_z, sin_z = host_tables(depth)
    table_x = np.concatenate([cos_x, sin_x], axis=0).astype(np.float32)
    forward_y = np.block([[cos_y, -sin_y], [sin_y, cos_y]]).astype(np.float32)
    inverse_y = np.block([[cos_y, sin_y], [-sin_y, cos_y]]).astype(np.float32)
    table_z = np.concatenate([cos_z, sin_z], axis=0).astype(np.float32)
    step = host_propagator(1, width_x, width_y)
    nearest = [depth - (s * local_depth + local_depth - 1) for s in range(slabs)]
    start = np.stack([host_propagator(d, width_x, width_y) for d in nearest])
    vmem, anywhere = pl.BlockSpec(memory_space=pltpu.VMEM), pl.BlockSpec(memory_space=pl.ANY)
    f32 = jnp.float32
    block = pltpu.VMEM((slabs, local_depth, cols_x, pair_y), f32)
    planes = pltpu.VMEM((local_depth, width_x, width_y), f32)
    padded = pltpu.VMEM((local_depth + 2 * passes, width_x, width_y), f32)
    turned = pltpu.VMEM((cols_x, depth, pair_y), f32)
    cols_table = pltpu.VMEM((pair_y, pair_y), jnp.bfloat16)
    rows_table = pltpu.VMEM((2 * width_x, width_x), jnp.bfloat16)
    several = pltpu.SemaphoreType.DMA((1, slabs))
    scattered, predicted, doubled = pl.pallas_call(
        fused_kernel,
        out_shape=(
            jax.ShapeDtypeStruct(field_now.shape, f32),
            jax.ShapeDtypeStruct(detector_data.shape, f32),
            jax.ShapeDtypeStruct(contrast.shape, f32),
        ),
        in_specs=[anywhere] * 10,
        out_specs=(vmem, vmem, vmem),
        scratch_shapes=[
            block, block, block, block,
            pltpu.VMEM((slabs, cols_x, pair_y), f32),
            planes, planes, padded, padded, turned, turned,
            pltpu.VMEM((width_x, pair_y), f32),
            pltpu.VMEM((width_x, width_y), f32),
            pltpu.VMEM(field_now.shape, f32),
            planes,
            pltpu.VMEM(forward_y.shape, f32),
            pltpu.VMEM(table_x.shape, f32),
            pltpu.VMEM(green_spectrum.shape, f32),
            pltpu.VMEM((width_x, pair_y), f32),
            pltpu.VMEM(detector_data.shape, f32),
            pltpu.VMEM(table_z.shape, f32),
            pltpu.VMEM((width_x, pair_y), f32),
            pltpu.VMEM(inverse_y.shape, f32),
            cols_table, cols_table, cols_table, cols_table, rows_table, rows_table,
            pltpu.VMEM((2 * depth, 4 * depth), jnp.bfloat16),
            pltpu.SemaphoreType.DMA((10,)),
            several, several, several, several, several, several,
            pltpu.SemaphoreType.DMA((local_depth,)),
            pltpu.SemaphoreType.DMA((local_depth,)),
            pltpu.SemaphoreType.DMA((2,)),
            pltpu.SemaphoreType.DMA((2,)),
        ],
        compiler_params=pltpu.CompilerParams(
            collective_id=0, has_side_effects=True, vmem_limit_bytes=60 * 2**20
        ),
    )(
        field_now, contrast, forward_y, table_x, green_spectrum, step,
        detector_data, table_z, start, inverse_y,
    )
    field_next = incident.astype(f32) + scattered
    return (field_next, predicted - detector_data, 0.5 * doubled)


def whole_tiles(mesh, arrays):
    local_depth = arrays[2].shape[0]
    rows = arrays[3].shape[2]
    return (
        mesh.shape["illum"] == 2
        and mesh.shape["slab"] > 1
        and rows % 8 == 0
        and (local_depth * mesh.shape["slab"]) % 16 == 0
        and arrays[2].shape[2] % 128 == 0
        and local_depth >= passes
    )


def solution(mesh):
    placed = (
        P("illum", None, "slab", None, None),
        P("illum", None, "slab", None, None),
        P("slab", None, None),
        P(None, None, "slab", None),
        P("illum", None, "slab", None),
    )

    def pick(*arrays):
        return (fused if whole_tiles(mesh, arrays) else shards)(*arrays)

    return jax.shard_map(
        pick,
        mesh=mesh,
        in_specs=placed,
        out_specs=(
            P("illum", None, "slab", None, None),
            P("illum", None, "slab", None),
            P("slab", None, None),
        ),
        check_vma=False,
    )
```

```python
import math

import jax
import jax.numpy as jnp
import numpy as np
from jax import lax
from jax.experimental import pallas as pl
from jax.experimental.pallas import tpu as pltpu
from jax.sharding import PartitionSpec as P

wave_number = 1.2
step_size = 2.0
diffusion = 0.02
edge_scale = 0.25
passes = 4
MESH = pl.DeviceIdType.MESH
highest = lax.Precision.HIGH
form_rows = "...xy,xk->...ky"
form_cols = "...y,yk->...k"
form_depth = "azxy,zk->akxy"


def with_halo(array, sides, width):
    for axis, dim in sides:
        devices, length = (lax.axis_size(axis), array.shape[dim])
        up = [(i, (i + 1) % devices) for i in range(devices - 1)]
        down = [(j, i) for i, j in up]
        last = lax.slice_in_dim(array, length - width, length, axis=dim)
        leading = lax.slice_in_dim(array, 0, width, axis=dim)
        before = lax.ppermute(last, axis, up)
        after = lax.ppermute(leading, axis, down)
        array = jnp.concatenate([before, array, after], axis=dim)
    return array


def tables(length):
    counter = jnp.arange(length, dtype=jnp.int32)
    product = counter[:, None] * counter[None, :] % length
    angle = product.astype(jnp.float32) * (2.0 * math.pi / length)
    scale = 1.0 / math.sqrt(length)
    return (jnp.cos(angle) * scale, jnp.sin(angle) * scale)


def mixing(real, imag, cosine, sine_table, sign, form):
    real_cos = jnp.einsum(form, real, cosine, precision=highest)
    real_sin = jnp.einsum(form, real, sine_table, precision=highest)
    imag_cos = jnp.einsum(form, imag, cosine, precision=highest)
    imag_sin = jnp.einsum(form, imag, sine_table, precision=highest)
    return (real_cos - sign * imag_sin, imag_cos + sign * real_sin)


def frequency(index, length):
    shifted = jnp.where(index < length // 2, index, index - length)
    return shifted.astype(jnp.float32) * (2.0 * math.pi / length)


def propagator(depth_index, row_index, width_x, width_y, depth):
    along_x = frequency(row_index, width_x)
    along_y = frequency(jnp.arange(width_y, dtype=jnp.int32), width_y)
    squared = wave_number**2 - along_x[None, :, None] ** 2 - along_y[None, None, :] ** 2
    distance = (depth - depth_index).astype(jnp.float32)[:, None, None]
    root = jnp.sqrt(jnp.abs(squared))
    moving = squared > 0.0
    amplitude = jnp.where(moving, 1.0, jnp.exp(-root * distance))
    phase = jnp.where(moving, root * distance, 0.0)
    return (amplitude * jnp.cos(phase), amplitude * jnp.sin(phase))


def tv_pass(padded, first, depth):
    rows = padded.shape[0]
    global_row = first + jnp.arange(rows - 1, dtype=jnp.int32)
    inside = (global_row >= 0) & (global_row <= depth - 2)
    core = padded[:-1]
    slope_depth = jnp.where(inside[:, None, None], padded[1:] - core, 0.0)
    slope_rows = jnp.concatenate([core[:, 1:] - core[:, :-1], jnp.zeros_like(core[:, :1])], axis=1)
    slope_cols = jnp.concatenate(
        [core[:, :, 1:] - core[:, :, :-1], jnp.zeros_like(core[:, :, :1])], axis=2
    )
    magnitude = jnp.sqrt(slope_depth**2 + slope_rows**2 + slope_cols**2 + edge_scale**2)
    flux_depth = slope_depth / magnitude
    flux_rows = (slope_rows / magnitude)[1:]
    flux_cols = (slope_cols / magnitude)[1:]
    spread_depth = flux_depth[1:] - flux_depth[:-1]
    spread_rows = flux_rows - jnp.concatenate(
        [jnp.zeros_like(flux_rows[:, :1]), flux_rows[:, :-1]], axis=1
    )
    spread_cols = flux_cols - jnp.concatenate(
        [jnp.zeros_like(flux_cols[:, :, :1]), flux_cols[:, :, :-1]], axis=2
    )
    return padded[1:-1] + diffusion * (spread_depth + spread_rows + spread_cols)


def back_project(prop_real, prop_imag, mismatch, root_depth):
    miss_real = mismatch[:, 0][:, None]
    miss_imag = mismatch[:, 1][:, None]
    out_real = (prop_real[None] * miss_real + prop_imag[None] * miss_imag) / root_depth
    out_imag = (prop_real[None] * miss_imag - prop_imag[None] * miss_real) / root_depth
    return jnp.stack([out_real, out_imag], 1)


def shards(incident, field_now, contrast, green_spectrum, detector_data):
    slabs = lax.axis_size("slab")
    place = lax.axis_index("slab")
    local_depth, width_x, width_y = contrast.shape
    depth = local_depth * slabs
    cols_x = width_x // slabs
    root_depth = math.sqrt(depth)
    cos_x, sin_x = tables(width_x)
    cos_y, sin_y = tables(width_y)
    cos_z, sin_z = tables(depth)
    real_now = field_now[:, 0]
    imag_now = field_now[:, 1]
    spec_real, spec_imag = mixing(
        contrast[None] * real_now, contrast[None] * imag_now, cos_x, sin_x, -1.0, form_rows
    )
    spec_real, spec_imag = mixing(spec_real, spec_imag, cos_y, sin_y, -1.0, form_cols)
    spectrum = jnp.stack([spec_real, spec_imag], 1)
    columns = lax.all_to_all(spectrum, "slab", split_axis=3, concat_axis=2, tiled=True)
    deep_real, deep_imag = mixing(columns[:, 0], columns[:, 1], cos_z, sin_z, -1.0, form_depth)
    green_real = green_spectrum[0][None]
    green_imag = green_spectrum[1][None]
    prod_real = green_real * deep_real - green_imag * deep_imag
    prod_imag = green_real * deep_imag + green_imag * deep_real
    vol_real, vol_imag = mixing(prod_real, prod_imag, cos_z, sin_z, 1.0, form_depth)
    volume = jnp.stack([vol_real, vol_imag], 1)
    kx_index = place * cols_x + jnp.arange(cols_x, dtype=jnp.int32)
    col_prop_real, col_prop_imag = propagator(
        jnp.arange(depth, dtype=jnp.int32), kx_index, width_x, width_y, depth
    )
    col_real = columns[:, 0]
    col_imag = columns[:, 1]
    pred_real = (
        jnp.sum(col_prop_real[None] * col_real - col_prop_imag[None] * col_imag, axis=1)
        / root_depth
    )
    pred_imag = (
        jnp.sum(col_prop_real[None] * col_imag + col_prop_imag[None] * col_real, axis=1)
        / root_depth
    )
    mismatch = jnp.stack([pred_real, pred_imag], 1) - detector_data
    volume = lax.all_to_all(volume, "slab", split_axis=2, concat_axis=3, tiled=True)
    depth_index = place * local_depth + jnp.arange(local_depth, dtype=jnp.int32)
    prop_real, prop_imag = propagator(
        depth_index, jnp.arange(width_x, dtype=jnp.int32), width_x, width_y, depth
    )
    gathered = lax.all_gather(mismatch, "slab", axis=2, tiled=True)
    returned = back_project(prop_real, prop_imag, gathered, root_depth)
    scat_real, scat_imag = mixing(volume[:, 0], volume[:, 1], cos_x, sin_x, 1.0, form_rows)
    scat_real, scat_imag = mixing(scat_real, scat_imag, cos_y, sin_y, 1.0, form_cols)
    field_next = incident.astype(jnp.float32) + jnp.stack([scat_real, scat_imag], 1)
    ret_real, ret_imag = mixing(returned[:, 0], returned[:, 1], cos_x, sin_x, 1.0, form_rows)
    ret_real, ret_imag = mixing(ret_real, ret_imag, cos_y, sin_y, 1.0, form_cols)
    local_terms = jnp.sum(real_now * ret_real + imag_now * ret_imag, axis=0)
    illums = lax.axis_size("illum")
    gradient, travelling = local_terms, local_terms
    for hop in range(illums - 1):
        travelling = lax.ppermute(travelling, "illum", [(i, (i + 1) % illums) for i in range(illums)])
        gradient = gradient + travelling
    updated = contrast - step_size * gradient
    wide = math.gcd(passes, local_depth)
    for repeat in range(passes // wide):
        updated = with_halo(updated, (("slab", 0),), wide)
        for left in range(wide, 0, -1):
            updated = tv_pass(updated, place * local_depth - left, depth)
    return (field_next, mismatch, updated)


def split_halves(value):
    high = value.astype(jnp.bfloat16)
    return high, (value - high.astype(jnp.float32)).astype(jnp.bfloat16)


def product(left, right):
    return jnp.dot(left, right, preferred_element_type=jnp.float32)


def combine(both, sign):
    rows, cols = both.shape[0] // 2, both.shape[1] // 2
    by_cos, by_sin = both[:rows], both[rows:]
    real = by_cos[:, :cols] - sign * by_sin[:, cols:]
    imag = by_cos[:, cols:] + sign * by_sin[:, :cols]
    return real, imag


def transform_rows(pair, high_ref, low_ref, sign):
    high, low = split_halves(pair)
    table = high_ref[...]
    both = product(table, high) + product(table, low) + product(low_ref[...], high)
    return jnp.concatenate(combine(both, sign), axis=1)


def transform_cols(pair, high_ref, low_ref):
    high, low = split_halves(pair)
    table = high_ref[...]
    return product(high, table) + product(low, table) + product(high, low_ref[...])


def host_tables(length):
    counter = np.arange(length)
    angle = (counter[:, None] * counter[None, :] % length) * (2.0 * math.pi / length)
    return np.cos(angle) / math.sqrt(length), np.sin(angle) / math.sqrt(length)


def host_frequency(length):
    index = np.arange(length)
    return np.where(index < length // 2, index, index - length) * (2.0 * math.pi / length)


def host_propagator(distance, width_x, width_y):
    squared = (
        wave_number**2 - host_frequency(width_x)[:, None] ** 2 - host_frequency(width_y)[None] ** 2
    )
    root = np.sqrt(np.abs(squared))
    moving = squared > 0.0
    amplitude = np.where(moving, 1.0, np.exp(-root * distance))
    phase = np.where(moving, root * distance, 0.0)
    pair = [amplitude * np.cos(phase), amplitude * np.sin(phase)]
    return np.concatenate(pair, axis=1).astype(np.float32)


def fused_kernel(
    field_any, contrast_any, yf_any, x_any, green_any, step_any,
    detector_any, z_any, start_any, yi_any,
    field_out, misfit_out, contrast_out,
    out1, in1, out2, in2, miss, gmine, gpeer, cube, cube2, zbuf, gbuf, rbuf, fz,
    field, contrast, yf, xt, green, step_ref, detector, zf, start, yi,
    yfh, yfl, yih, yil, xh, xl, zt_ref,
    load_sem, s1, r1, s2, r2, sm, rm, sg, rg, sh, rh,
):
    slabs, local_depth, cols_x, pair_y = out1.shape
    width_y = pair_y // 2
    width_x = slabs * cols_x
    depth = slabs * local_depth
    root_depth = math.sqrt(depth)
    me = lax.axis_index("slab")
    lane = lax.axis_index("illum")
    other = 1 - lane

    def at(hop):
        return lax.rem(me + hop, slabs)

    def far_first(hop):
        return lax.rem(hop + slabs // 2 - 1, slabs - 1) + 1

    def spread(body):
        lax.fori_loop(1, slabs, lambda hop, carry: (body(at(far_first(hop))), carry)[1], 0)

    barrier = pltpu.get_barrier_semaphore()

    def greet(dst):
        pl.semaphore_signal(barrier, inc=1, device_id=(lane, dst), device_id_type=MESH)

    sources = [
        field_any, contrast_any, yf_any, x_any, green_any, step_any,
        detector_any, z_any, start_any.at[me], yi_any,
    ]
    held = [field, contrast, yf, xt, green, step_ref, detector, zf, start, yi]
    early = 4
    loads = [
        pltpu.make_async_copy(src, dst, load_sem.at[i])
        for i, (src, dst) in enumerate(zip(sources, held))
    ]
    for load in loads:
        load.start()
    spread(greet)
    pl.semaphore_signal(barrier, inc=1, device_id=(other, me), device_id_type=MESH)

    def remote(src, dst, send, recv, who):
        return pltpu.make_async_remote_copy(
            src_ref=src, dst_ref=dst, send_sem=send, recv_sem=recv,
            device_id=who, device_id_type=MESH,
        )

    def forward(plane, carry):
        c = contrast[plane]
        pair = jnp.concatenate([c * field[0, 0, plane], c * field[0, 1, plane]], axis=1)
        pair = transform_cols(pair, yfh, yfl)
        pair = transform_rows(pair, xh, xl, -1.0)
        out1[:, plane] = pair.reshape(slabs, cols_x, pair_y)
        return carry

    for load in loads[:early]:
        load.wait()
    yfh[...], yfl[...] = split_halves(yf[...])
    xh[...], xl[...] = split_halves(xt[...])
    parts = 1
    groups = math.gcd(local_depth, 2)
    size = local_depth // groups

    def send_block(part, first, count):
        planes, rows = pl.ds(first, count), pl.ds(0, cols_x)
        spread(
            lambda dst: remote(
                out1.at[dst, planes, rows], in1.at[me, planes, rows],
                s1.at[part, dst], r1.at[part, me], (lane, dst),
            ).start()
        )

    for group in range(groups):
        lax.fori_loop(group * size, (group + 1) * size, forward, 0)
        if group == 0:
            pl.semaphore_wait(barrier, slabs)
        send_block(0, group * size, size)
    for part in range(1, parts):
        send_block(part, 0, local_depth)
    in1[me] = out1[me]

    for load in loads[early:]:
        load.wait()
    yih[...], yil[...] = split_halves(yi[...])
    z_high, z_low = split_halves(zf[...])
    zt_ref[...] = jnp.concatenate([z_high, z_high, z_low, z_low], axis=1)
    for first in range(0, cols_x, 8):
        rows = slice(first, first + 8)
        for half in range(2):
            cols = slice(half * width_y, (half + 1) * width_y)
            gbuf[rows, :, cols] = jnp.transpose(green[half, :, rows, :], (1, 0, 2))

    def convolve(row, carry):
        table = zt_ref[...]
        high, low = split_halves(zbuf[row])
        both = product(table, jnp.concatenate([high, low, high, low], axis=0))
        real, imag = combine(both, -1.0)
        g_real, g_imag = gbuf[row, :, :width_y], gbuf[row, :, width_y:]
        pair = jnp.concatenate(
            [g_real * real - g_imag * imag, g_real * imag + g_imag * real], axis=1
        )
        high, low = split_halves(pair)
        both = product(table, jnp.concatenate([high, low, high, low], axis=0))
        zbuf[row] = jnp.concatenate(combine(both, 1.0), axis=1)
        return carry

    for part in range(parts):
        rows, cut = slice(0, cols_x), pl.ds(0, cols_x)
        spread(
            lambda src: remote(
                out1.at[src, :, cut], in1.at[src, :, cut],
                s1.at[part, src], r1.at[part, src], (lane, src),
            ).wait_recv()
        )
        own = pl.ds(pl.multiple_of(me * cols_x, 8), cols_x)
        step_r, step_i = step_ref[own, :width_y], step_ref[own, width_y:]

        def horner(src, carry):
            real, imag = carry
            for plane in range(local_depth):
                real = real + in1[src, plane, rows, :width_y]
                imag = imag + in1[src, plane, rows, width_y:]
                real, imag = (real * step_r - imag * step_i, real * step_i + imag * step_r)
            return real, imag

        zero = jnp.zeros((cols_x, width_y), jnp.float32)
        real, imag = lax.fori_loop(0, slabs, horner, (zero, zero))
        real = real / root_depth
        imag = imag / root_depth
        misfit_out[0, 0, rows] = real
        misfit_out[0, 1, rows] = imag
        real = real - detector[0, 0, rows]
        imag = imag - detector[0, 1, rows]
        miss[me, rows, :width_y] = real
        miss[me, rows, width_y:] = imag
        spread(
            lambda dst: remote(
                miss.at[me, cut], miss.at[me, cut],
                sm.at[part, dst], rm.at[part, me], (lane, dst),
            ).start()
        )
        for first in range(0, cols_x, 8):
            eight = slice(first, first + 8)
            block = in1[:, :, eight, :].reshape(depth, 8, pair_y)
            zbuf[eight] = jnp.transpose(block, (1, 0, 2))
        lax.fori_loop(0, cols_x, convolve, 0)
        for first in range(0, cols_x, 8):
            eight = slice(first, first + 8)
            block = jnp.transpose(zbuf[eight], (1, 0, 2))
            out2[:, :, eight, :] = block.reshape(slabs, local_depth, 8, pair_y)
        spread(
            lambda dst: remote(
                out2.at[dst, :, cut], in2.at[me, :, cut],
                s2.at[part, dst], r2.at[part, me], (lane, dst),
            ).start()
        )
    in2[me] = out2[me]

    for part in range(parts):
        cut = pl.ds(0, cols_x)
        spread(
            lambda src: remote(
                miss.at[src, cut], miss.at[src, cut],
                sm.at[part, src], rm.at[part, src], (lane, src),
            ).wait_recv()
        )
    gathered = miss[...].reshape(width_x, pair_y)
    m_real, m_imag = gathered[:, :width_y], gathered[:, width_y:]
    p_real, p_imag = start[:, :width_y], start[:, width_y:]
    rbuf[:, :width_y] = (p_real * m_real + p_imag * m_imag) / root_depth
    rbuf[:, width_y:] = (p_real * m_imag - p_imag * m_real) / root_depth

    def peer_copy(plane):
        return remote(
            gmine.at[plane], gpeer.at[plane], sg.at[plane], rg.at[plane], (other, me)
        )

    def project(count, carry):
        plane = local_depth - 1 - count
        now = rbuf[...]
        pair = transform_rows(now, xh, xl, 1.0)
        pair = transform_cols(pair, yih, yil)
        gmine[plane] = field[0, 0, plane] * pair[:, :width_y] + field[0, 1, plane] * pair[:, width_y:]
        peer_copy(plane).start()
        now_r, now_i = now[:, :width_y], now[:, width_y:]
        w_real, w_imag = step_ref[:, :width_y], step_ref[:, width_y:]
        rbuf[:, :width_y] = w_real * now_r + w_imag * now_i
        rbuf[:, width_y:] = w_real * now_i - w_imag * now_r
        return carry

    lax.fori_loop(0, local_depth, project, 0)

    def update(count, carry):
        plane = local_depth - 1 - count
        peer_copy(plane).wait()
        cube[passes + plane] = contrast[plane] - step_size * (gmine[plane] + gpeer[plane])
        return carry

    lax.fori_loop(0, local_depth, update, 0)
    low_side, high_side = pl.ds(0, passes), pl.ds(passes + local_depth, passes)
    up = remote(
        cube.at[pl.ds(local_depth, passes)], cube.at[low_side], sh.at[0], rh.at[0],
        (lane, lax.rem(me + 1, slabs)),
    )
    down = remote(
        cube.at[pl.ds(passes, passes)], cube.at[high_side], sh.at[1], rh.at[1],
        (lane, lax.rem(me + slabs - 1, slabs)),
    )
    has_up, has_down = me < slabs - 1, me > 0
    pl.when(has_up)(up.start)
    pl.when(has_down)(down.start)

    @pl.when(me == 0)
    def _():
        cube[low_side] = jnp.zeros((passes, width_x, width_y), jnp.float32)

    @pl.when(me == slabs - 1)
    def _():
        cube[high_side] = jnp.zeros((passes, width_x, width_y), jnp.float32)

    for part in range(parts):
        cut = pl.ds(0, cols_x)
        spread(
            lambda src: remote(
                out2.at[src, :, cut], in2.at[src, :, cut],
                s2.at[part, src], r2.at[part, src], (lane, src),
            ).wait_recv()
        )

    def finish(plane, carry):
        pair = in2[:, plane].reshape(width_x, pair_y)
        pair = transform_rows(pair, xh, xl, 1.0)
        pair = transform_cols(pair, yih, yil)
        field_out[0, 0, plane] = pair[:, :width_y]
        field_out[0, 1, plane] = pair[:, width_y:]
        return carry

    lax.fori_loop(0, local_depth, finish, 0)

    pl.when(has_up)(up.wait_send)
    pl.when(has_down)(down.wait_send)
    pl.when(has_down)(up.wait_recv)
    pl.when(has_up)(down.wait_recv)

    row_at = lax.broadcasted_iota(jnp.int32, (width_x, width_y), 0)
    col_at = lax.broadcasted_iota(jnp.int32, (width_x, width_y), 1)

    def sweep(source, plane, write):
        cur = source[plane]
        place = me * local_depth - passes + plane
        inside = jnp.where((place >= 0) & (place <= depth - 2), 1.0, 0.0)
        slope_z = (source[plane + 1] - cur) * inside
        flux_x = jnp.where(row_at < width_x - 1, pltpu.roll(cur, width_x - 1, 0) - cur, 0.0)
        flux_y = jnp.where(col_at < width_y - 1, pltpu.roll(cur, width_y - 1, 1) - cur, 0.0)
        scale = lax.rsqrt(slope_z**2 + flux_x**2 + flux_y**2 + edge_scale**2)
        flux_z = slope_z * scale
        if write is not None:
            flux_x = flux_x * scale
            flux_y = flux_y * scale
            total = flux_z - fz[...] + flux_x - pltpu.roll(flux_x, 1, 0)
            total = total + flux_y - pltpu.roll(flux_y, 1, 1)
            write(plane, cur + diffusion * total)
        fz[...] = flux_z

    planes = local_depth + 2 * passes
    for turn in range(passes):
        source, target = (cube, cube2) if turn % 2 == 0 else (cube2, cube)
        sweep(source, turn, None)

        def write(plane, value, turn=turn, target=target):
            if turn == passes - 1:
                contrast_out[plane - passes] = 2.0 * value
            else:
                target[plane] = value

        def one(plane, carry, source=source, write=write):
            sweep(source, plane, write)
            return carry

        lax.fori_loop(turn + 1, planes - 1 - turn, one, 0)

    def drain(part, dst):
        cut = pl.ds(0, cols_x)
        who = (lane, dst)
        remote(
            out1.at[dst, :, cut], in1.at[me, :, cut], s1.at[part, dst], r1.at[part, me], who
        ).wait_send()
        remote(
            miss.at[me, cut], miss.at[me, cut], sm.at[part, dst], rm.at[part, me], who
        ).wait_send()
        remote(
            out2.at[dst, :, cut], in2.at[me, :, cut], s2.at[part, dst], r2.at[part, me], who
        ).wait_send()

    for part in range(parts):
        spread(lambda dst: drain(part, dst))


def fused(incident, field_now, contrast, green_spectrum, detector_data):
    slabs = lax.axis_size("slab")
    local_depth, width_x, width_y = contrast.shape
    depth = local_depth * slabs
    cols_x = width_x // slabs
    pair_y = 2 * width_y
    cos_x, sin_x = host_tables(width_x)
    cos_y, sin_y = host_tables(width_y)
    cos_z, sin_z = host_tables(depth)
    table_x = np.concatenate([cos_x, sin_x], axis=0).astype(np.float32)
    forward_y = np.block([[cos_y, -sin_y], [sin_y, cos_y]]).astype(np.float32)
    inverse_y = np.block([[cos_y, sin_y], [-sin_y, cos_y]]).astype(np.float32)
    table_z = np.concatenate([cos_z, sin_z], axis=0).astype(np.float32)
    step = host_propagator(1, width_x, width_y)
    nearest = [depth - (s * local_depth + local_depth - 1) for s in range(slabs)]
    start = np.stack([host_propagator(d, width_x, width_y) for d in nearest])
    vmem, anywhere = pl.BlockSpec(memory_space=pltpu.VMEM), pl.BlockSpec(memory_space=pl.ANY)
    f32 = jnp.float32
    block = pltpu.VMEM((slabs, local_depth, cols_x, pair_y), f32)
    planes = pltpu.VMEM((local_depth, width_x, width_y), f32)
    padded = pltpu.VMEM((local_depth + 2 * passes, width_x, width_y), f32)
    turned = pltpu.VMEM((cols_x, depth, pair_y), f32)
    cols_table = pltpu.VMEM((pair_y, pair_y), jnp.bfloat16)
    rows_table = pltpu.VMEM((2 * width_x, width_x), jnp.bfloat16)
    several = pltpu.SemaphoreType.DMA((1, slabs))
    scattered, predicted, doubled = pl.pallas_call(
        fused_kernel,
        out_shape=(
            jax.ShapeDtypeStruct(field_now.shape, f32),
            jax.ShapeDtypeStruct(detector_data.shape, f32),
            jax.ShapeDtypeStruct(contrast.shape, f32),
        ),
        in_specs=[anywhere] * 10,
        out_specs=(vmem, vmem, vmem),
        scratch_shapes=[
            block, block, block, block,
            pltpu.VMEM((slabs, cols_x, pair_y), f32),
            planes, planes, padded, padded, turned, turned,
            pltpu.VMEM((width_x, pair_y), f32),
            pltpu.VMEM((width_x, width_y), f32),
            pltpu.VMEM(field_now.shape, f32),
            planes,
            pltpu.VMEM(forward_y.shape, f32),
            pltpu.VMEM(table_x.shape, f32),
            pltpu.VMEM(green_spectrum.shape, f32),
            pltpu.VMEM((width_x, pair_y), f32),
            pltpu.VMEM(detector_data.shape, f32),
            pltpu.VMEM(table_z.shape, f32),
            pltpu.VMEM((width_x, pair_y), f32),
            pltpu.VMEM(inverse_y.shape, f32),
            cols_table, cols_table, cols_table, cols_table, rows_table, rows_table,
            pltpu.VMEM((2 * depth, 4 * depth), jnp.bfloat16),
            pltpu.SemaphoreType.DMA((10,)),
            several, several, several, several, several, several,
            pltpu.SemaphoreType.DMA((local_depth,)),
            pltpu.SemaphoreType.DMA((local_depth,)),
            pltpu.SemaphoreType.DMA((2,)),
            pltpu.SemaphoreType.DMA((2,)),
        ],
        compiler_params=pltpu.CompilerParams(
            collective_id=0, has_side_effects=True, vmem_limit_bytes=60 * 2**20
        ),
    )(
        field_now, contrast, forward_y, table_x, green_spectrum, step,
        detector_data, table_z, start, inverse_y,
    )
    field_next = incident.astype(f32) + scattered
    return (field_next, predicted - detector_data, 0.5 * doubled)


def whole_tiles(mesh, arrays):
    local_depth = arrays[2].shape[0]
    rows = arrays[3].shape[2]
    return (
        mesh.shape["illum"] == 2
        and mesh.shape["slab"] > 1
        and rows % 8 == 0
        and (local_depth * mesh.shape["slab"]) % 16 == 0
        and arrays[2].shape[2] % 128 == 0
        and local_depth >= passes
    )


def solution(mesh):
    placed = (
        P("illum", None, "slab", None, None),
        P("illum", None, "slab", None, None),
        P("slab", None, None),
        P(None, None, "slab", None),
        P("illum", None, "slab", None),
    )

    def pick(*arrays):
        return (fused if whole_tiles(mesh, arrays) else shards)(*arrays)

    return jax.shard_map(
        pick,
        mesh=mesh,
        in_specs=placed,
        out_specs=(
            P("illum", None, "slab", None, None),
            P("illum", None, "slab", None),
            P("slab", None, None),
        ),
        check_vma=False,
    )
```
